256 devices in a mesh: tm: 16 (over y, z_lo, core), dp: 4 (over z_hi), factor: 4 (over x).
Axes of the slice: x: 4, y: 4, z: 8 (z_hi: 4, z_lo: 2; z = z_hi * 2 + z_lo), core: 2. Of those that a mesh axis runs over, the one named last changes fastest.
Arguments:
- activations: bfloat16 [65536, 1280], P(('tm', 'dp'), 'factor'), may hold values from -16 to 16
- gradients: bfloat16 [65536, 2560], P(('tm', 'dp'), 'factor'), may hold values from -16 to 16
- valid_frames: int32 [65536], P(('tm', 'dp')), may hold values from 0 to 1, as said below
- basis_in: bfloat16 [1280, 1280], replicated, may hold values from -0.15625 to 0.15625
- basis_out: bfloat16 [2560, 2560], P(None, 'factor'), may hold values from -0.125 to 0.125
- eigen_in: float32 [1280], replicated, may hold values from 0.01 to 0.3
- eigen_out: float32 [2560], replicated, may hold values from 0.01 to 0.3
- previous_in: float32 [1280, 1280], P(('tm', 'dp', 'factor')), may hold values from -0.6 to 1.5
- previous_out: float32 [2560, 2560], P(('tm', 'dp', 'factor')), may hold values from -0.6 to 1.5
Outputs:
- factor_in: float32 [1280, 1280], P(('tm', 'dp', 'factor'))
- factor_out: float32 [2560, 2560], P(('tm', 'dp', 'factor'))
- preconditioned: bfloat16 [2560, 1280], P(('tm', 'dp', 'factor'))
The draws below stay inside these ranges and needn't reach their ends.
Inputs may be any that keep to these rules, and one draw needn't show every extreme that they name: `valid_frames`: in each block of 1024 frames, the frames before a drawn length (a third of the block or more) are 1 and the rest 0.
All inputs are finite; a program needn't handle non-finite values.
Results may differ from the reference program's by a relative error of at most 0.009.
Values may be sent and summed in bfloat16 or wider, within the bound.
A program may use at most 128 MiB of HBM per device.

```python
import math
import jax
import jax.numpy as jnp

D = 1280
C = 2560
FR_DEV = 1024
FRAMES = 65536


def draw_valid_frames(key, part):
    key = jax.random.fold_in(key, 11)
    blocks = FRAMES // FR_DEV
    lengths = jax.random.randint(key, (blocks, 1), FR_DEV // 3 + 1, FR_DEV + 1)
    where = jnp.arange(FR_DEV, dtype=jnp.int32)[None, :]
    return (where < lengths).astype(jnp.int32).reshape(FRAMES)


def channel_mix(key, noise, column_scale):
    width = noise.shape[1]
    keys = jax.random.split(key, 4)
    combined = 2.0 * noise
    for repeat in range(3):
        order = jax.random.permutation(keys[repeat], width)
        combined = combined + noise[:, order]
    combined = combined * (column_scale[None, :] / math.sqrt(7.0))
    blocks = FRAMES // FR_DEV
    pairing = jax.random.permutation(keys[3], blocks)
    span = width // blocks
    channel_block = jnp.arange(width, dtype=jnp.int32) // span
    frame_block = jnp.arange(FRAMES, dtype=jnp.int32) // FR_DEV
    owner_block = pairing[frame_block]
    struck = channel_block[None, :] == owner_block[:, None]
    combined = jnp.where(struck, 5.0 * combined, combined)
    return jnp.clip(combined, -16.0, 16.0)


def symmetric_factor(key, width):
    keys = jax.random.split(key, 2)
    noise = 0.15 * jax.random.truncated_normal(keys[0], -4.0, 4.0, (width, width), jnp.float32)
    paired = 0.5 * (noise + noise.T)
    diagonal_values = jax.random.uniform(keys[1], (width,), jnp.float32, 0.5, 1.5)
    places = jnp.arange(width, dtype=jnp.int32)
    on_diagonal = places[:, None] == places[None, :]
    return jnp.where(on_diagonal, diagonal_values[:, None], paired)


def draw_activations(key, part):
    key = jax.random.fold_in(key, 21)
    noise_key = jax.random.fold_in(key, 0)
    mix_key = jax.random.fold_in(key, 2)
    noise = jax.random.truncated_normal(noise_key, -4.0, 4.0, (FRAMES, D), jnp.float32)
    column_scale = jnp.ones((D,), jnp.float32)
    return channel_mix(mix_key, noise, column_scale).astype(jnp.bfloat16)


def draw_gradients(key, part):
    key = jax.random.fold_in(key, 23)
    noise_key = jax.random.fold_in(key, 0)
    mix_key = jax.random.fold_in(key, 2)
    noise = jax.random.truncated_normal(noise_key, -4.0, 4.0, (FRAMES, C), jnp.float32)
    column_scale = jnp.ones((C,), jnp.float32)
    return channel_mix(mix_key, noise, column_scale).astype(jnp.bfloat16)


def draw_previous_in(key, part):
    key = jax.random.fold_in(key, 31)
    return symmetric_factor(key, D)


def draw_previous_out(key, part):
    key = jax.random.fold_in(key, 37)
    return symmetric_factor(key, C)


def level_of(own_key, dims, pieces, least, high):
    level = 1.0
    for axis_at, shards_of in pieces:
        steps = jax.random.uniform(jax.random.fold_in(jax.random.fold_in(own_key, 6), axis_at), (shards_of,), jnp.float32, least / len(pieces), high / len(pieces))
        level = level * jnp.repeat(jnp.exp(steps), dims[axis_at] // shards_of).reshape((-1,) + (1,) * (len(dims) - 1 - axis_at))
    return level


def scatter_about(own_key, extent, deviation, limit, cuts=(), held_as=jnp.bfloat16):
    drawn = deviation * jax.random.normal(own_key, extent, jnp.float32)
    if cuts:
        drawn = drawn * level_of(own_key, extent, cuts, -0.22, 0.18)
    return jnp.clip(drawn, -limit, limit).astype(held_as)


def setup_inputs(seed: int = 0) -> dict:
    arg_keys = jax.random.split(jax.random.key(seed), 10)
    activations = draw_activations(jax.random.fold_in(arg_keys[9], 71), 0)
    gradients = draw_gradients(jax.random.fold_in(arg_keys[9], 71), 0)
    valid_frames = draw_valid_frames(jax.random.fold_in(arg_keys[9], 71), 0)
    basis_in = scatter_about(arg_keys[3], (D, D), D ** -0.5, 0.15625)
    basis_out = scatter_about(arg_keys[4], (C, C), C ** -0.5, 0.125, ((1, 4),))
    eigen_in = jnp.clip(jnp.exp(jax.random.uniform(arg_keys[5], (D,), jnp.float32, math.log(0.01), math.log(0.3))), 0.01, 0.3)
    eigen_out = jnp.clip(jnp.exp(jax.random.uniform(arg_keys[6], (C,), jnp.float32, math.log(0.01), math.log(0.3))), 0.01, 0.3)
    previous_in = draw_previous_in(jax.random.fold_in(arg_keys[9], 71), 0)
    previous_out = draw_previous_out(jax.random.fold_in(arg_keys[9], 71), 0)
    return dict(activations=activations, gradients=gradients, valid_frames=valid_frames, basis_in=basis_in, basis_out=basis_out, eigen_in=eigen_in, eigen_out=eigen_out, previous_in=previous_in, previous_out=previous_out)


factor_decay = 0.5
damping = 0.001


def reference(activations, gradients, valid_frames, basis_in, basis_out, eigen_in, eigen_out, previous_in, previous_out):
    weights = valid_frames.astype(jnp.bfloat16)[:, None]
    masked_acts = activations * weights
    masked_grads = gradients * weights
    frame_count = jnp.sum(valid_frames.astype(jnp.float32))
    gram_in = jnp.dot(masked_acts.T, masked_acts, preferred_element_type=jnp.float32)
    gram_out = jnp.dot(masked_grads.T, masked_grads, preferred_element_type=jnp.float32)
    factor_in = factor_decay * previous_in + (1.0 - factor_decay) * (gram_in / frame_count)
    factor_out = factor_decay * previous_out + (1.0 - factor_decay) * (gram_out / frame_count)
    rotated_in = jnp.dot(masked_acts, basis_in, preferred_element_type=jnp.float32).astype(jnp.bfloat16)
    rotated_out = jnp.dot(masked_grads, basis_out, preferred_element_type=jnp.float32).astype(jnp.bfloat16)
    rotated = jnp.dot(rotated_out.T, rotated_in, preferred_element_type=jnp.float32) / frame_count
    scaled = (rotated / (eigen_out[:, None] * eigen_in[None, :] + damping)).astype(jnp.bfloat16)
    back = jnp.dot(scaled, basis_in.T, preferred_element_type=jnp.float32).astype(jnp.bfloat16)
    preconditioned = jnp.dot(basis_out, back, preferred_element_type=jnp.float32).astype(jnp.bfloat16)
    return factor_in, factor_out, preconditioned
```

```python
import functools

import jax
import jax.numpy as jnp
from jax import lax
from jax.experimental import pallas as pl
from jax.experimental.pallas import tpu as pltpu
from jax.sharding import PartitionSpec as P

factor_decay = 0.5
damping = 0.001
MESH = pl.DeviceIdType.MESH
F32 = jnp.float32
BF16 = jnp.bfloat16

FR = 1024
WA = 320
WG = 640
MESSAGES = 128


def device(x, y, z, c):
    return {"tm": y * 4 + (z % 2) * 2 + c, "dp": z // 2, "factor": x}


def dot(left, right):
    return jnp.dot(left, right, preferred_element_type=F32)


def dot_nt(left, right):
    return lax.dot_general(left, right, (((1,), (1,)), ((), ())), preferred_element_type=F32)


def kernel(
    at_ref, g_ref, valid_ref, bi_ref, bo_ref, eo_ref, ei_ref, prev_in_ref, prev_out_ref,
    fin_ref, fout_ref, pre_ref,
    a_all, g_all, gt, bi, bo, bit,
    keep, c_send, c_recv, y_send, y_recv, z_send, z_recv, o_send, o_recv, i_send, i_recv,
    m_keep, mc_send, mc_recv, my_send, my_recv, mz_send, mz_recv, mx, wz, wy, wc,
    st, bt, px_send, px_recv,
    n_c, n_y, n_z, n_total,
    send_sem, recv_sem, load_sem,
):
    tm, dp, x = lax.axis_index("tm"), lax.axis_index("dp"), lax.axis_index("factor")
    y, c = tm // 4, tm % 2
    z = dp * 2 + (tm // 2) % 2
    group = tm * 4 + dp
    unit = group * 4 + x
    left, right, opposite = (x + 3) % 4, (x + 1) % 4, (x + 2) % 4

    def peer(dx=0, dy=0, dz=0, dc=0):
        return device((x + dx) % 4, (y + dy) % 4, (z + dz) % 8, (c + dc) % 2)

    out_unit = 64 * x + 32 * c + 8 * y + z
    out_dst = {"tm": out_unit // 16, "dp": (out_unit // 4) % 4, "factor": out_unit % 4}
    out_src = device(unit // 64, (unit // 8) % 4, unit % 8, (unit // 32) % 2)
    in_unit = [64 * x + 16 * y + 2 * z + h for h in range(2)]
    in_dst = [{"tm": u // 16, "dp": (u // 4) % 4, "factor": u % 4} for u in in_unit]
    in_src = [device(unit // 64, (unit // 16) % 4, (unit // 2) % 8, h) for h in range(2)]

    def same(d):
        return (d["tm"] == tm) & (d["dp"] == dp) & (d["factor"] == x)

    load_bi = pltpu.make_async_copy(bi_ref, bi, load_sem.at[0])
    load_bo = pltpu.make_async_copy(bo_ref, bo, load_sem.at[1])
    load_bi.start()
    load_bo.start()

    barrier = pltpu.get_barrier_semaphore()
    peers = [peer(dx=i) for i in (1, 2, 3)] + [peer(dy=i) for i in (1, 2, 3)]
    peers += [peer(dz=i) for i in range(1, 8)] + [peer(dc=1)]
    for d in peers:
        pl.semaphore_signal(barrier, inc=1, device_id=d, device_id_type=MESH)
    for d in [out_src] + in_src:

        @pl.when(jnp.logical_not(same(d)))
        def _():
            pl.semaphore_signal(barrier, inc=1, device_id=d, device_id_type=MESH)

    expected = len(peers)
    for d in [out_dst] + in_dst:
        expected = expected + jnp.where(same(d), 0, 1)

    length = jnp.sum(valid_ref[...], keepdims=True)
    a_all[x] = jnp.where(
        lax.broadcasted_iota(jnp.int32, (WA, FR), 1) < length, at_ref[...], jnp.zeros((), BF16)
    )
    n_c[0] = jnp.broadcast_to(length.astype(F32), (8, 128))
    pl.semaphore_wait(barrier, expected)

    count = [0]
    started = []

    def fresh():
        count[0] += 1
        return count[0] - 1

    def send(src, dst, to, k):
        copy = pltpu.make_async_remote_copy(
            src_ref=src, dst_ref=dst, send_sem=send_sem.at[k], recv_sem=recv_sem.at[k],
            device_id=to, device_id_type=MESH,
        )
        copy.start()
        started.append(copy)

    def landed(dst, k):
        pltpu.make_async_remote_copy(
            src_ref=dst, dst_ref=dst, send_sem=send_sem.at[k], recv_sem=recv_sem.at[k],
            device_id=peer(dx=1), device_id_type=MESH,
        ).wait_recv()

    class Gather:
        def __init__(self, buf, half):
            self.buf, self.h = buf, half
            self.k = [fresh() for _ in range(6)]

        def part(self, shard, h):
            return self.buf.at[shard, pl.ds(h * self.h, self.h)]

        def open(self):
            own0, own1 = self.part(x, 0), self.part(x, 1)
            send(own0, own0, peer(dx=1), self.k[0])
            send(own1, own1, peer(dx=3), self.k[2])
            send(own1, own1, peer(dx=1), self.k[1])
            send(own0, own0, peer(dx=3), self.k[3])

        def forward(self):
            landed(self.part(left, 0), self.k[0])
            send(self.part(left, 0), self.part(left, 0), peer(dx=1), self.k[4])
            landed(self.part(right, 1), self.k[2])
            send(self.part(right, 1), self.part(right, 1), peer(dx=3), self.k[5])

        def near_left(self):
            landed(self.part(left, 1), self.k[1])

        def near_right(self):
            landed(self.part(right, 0), self.k[3])

        def far(self):
            landed(self.part(opposite, 0), self.k[4])
            landed(self.part(opposite, 1), self.k[5])

    acts = Gather(a_all, WA // 2)
    grads = Gather(g_all, FR // 2)
    acts.open()

    kc, ky, kz = fresh(), [fresh() for _ in range(3)], [fresh() for _ in range(7)]
    send(n_c.at[0], n_c.at[1], peer(dc=1), kc)

    def count_y():
        landed(n_c.at[1], kc)
        n_y[0] = n_c[0] + n_c[1]
        for i in range(3):
            send(n_y.at[0], n_y.at[i + 1], peer(dy=i + 1), ky[i])

    def count_z():
        for i in range(3):
            landed(n_y.at[i + 1], ky[i])
        n_z[0] = n_y[0] + n_y[1] + n_y[2] + n_y[3]
        for i in range(7):
            send(n_z.at[0], n_z.at[i + 1], peer(dz=i + 1), kz[i])

    def count_done():
        for i in range(7):
            landed(n_z.at[i + 1], kz[i])
        total = n_z[0]
        for i in range(7):
            total = total + n_z[i + 1]
        n_total[...] = total

    class Scatter:
        def __init__(self, b):
            self.b = b
            self.kc = fresh()
            self.ky = [fresh() for _ in range(3)]
            self.kz = [fresh() for _ in range(7)]

        def core(self, half):
            b = self.b
            c_send[b] = half(1 - c).astype(BF16)
            send(c_send.at[b], c_recv.at[b], peer(dc=1), self.kc)
            keep[b] = half(c)

        def along_y(self):
            b = self.b
            landed(c_recv.at[b], self.kc)
            total = keep[b] + c_recv[b].astype(F32)
            keep[b] = total
            y_send[b] = total.astype(BF16)
            for i in range(3):
                to = (y + i + 1) % 4
                send(
                    y_send.at[b, pl.ds(pl.multiple_of(to * 80, 16), 80)],
                    y_recv.at[b, i], peer(dy=i + 1), self.ky[i],
                )

        def along_z(self):
            b = self.b
            total = keep[b, pl.ds(pl.multiple_of(y * 80, 16), 80)]
            for i in range(3):
                landed(y_recv.at[b, i], self.ky[i])
                total = total + y_recv[b, i].astype(F32)
            for i in range(8):
                z_send[b, i, :10] = total[10 * i : 10 * i + 10].astype(BF16)
            for i in range(7):
                send(z_send.at[b, (z + i + 1) % 8], z_recv.at[b, i], peer(dz=i + 1), self.kz[i])

        def done(self):
            b = self.b
            total = z_send[b, z].astype(F32)
            for i in range(7):
                landed(z_recv.at[b, i], self.kz[i])
                total = total + z_recv[b, i].astype(F32)
            return total

    blocks = [Scatter(i) for i in range(5)]
    ko = [fresh() for _ in range(4)]
    ki_send = [fresh() for _ in range(2)]
    ki = [fresh() for _ in range(2)]

    def out_copy(i):
        return pltpu.make_async_remote_copy(
            src_ref=o_send.at[i], dst_ref=o_recv.at[i], send_sem=send_sem.at[ko[i]],
            recv_sem=recv_sem.at[ko[i]], device_id=out_dst, device_id_type=MESH,
        )

    def hand_out(i, shard):
        o_send[i] = blocks[i].done()
        self_dst = same(out_dst)

        @pl.when(self_dst)
        def _():
            o_recv[i] = o_send[i]

        @pl.when(jnp.logical_not(self_dst))
        def _():
            out_copy(i).start()

    def in_copy(h):
        return pltpu.make_async_remote_copy(
            src_ref=i_send.at[h], dst_ref=i_recv.at[c], send_sem=send_sem.at[ki_send[h]],
            recv_sem=recv_sem.at[ki[0] + c], device_id=in_dst[h], device_id_type=MESH,
        )

    def hand_in():
        total = blocks[4].done()
        for h in range(2):
            i_send[h, :5] = total[5 * h : 5 * h + 5]
        for h in range(2):
            self_dst = same(in_dst[h])

            @pl.when(self_dst)
            def _(h=h):
                i_recv[c] = i_send[h]

            @pl.when(jnp.logical_not(self_dst))
            def _(h=h):
                in_copy(h).start()

    def out_block(shard):
        def half(h):
            rows = gt[pl.ds(pl.multiple_of(h * 320, 16), 320)]
            return dot(rows, g_all[shard])

        return half

    def in_block(h):
        other = a_all[pl.ds(2 * h, 2)].reshape(2 * WA, FR)
        return dot_nt(a_all[x], other)

    g_all[x] = jnp.where(
        lax.broadcasted_iota(jnp.int32, (FR, WG), 0) < length, g_ref[...], jnp.zeros((), BF16)
    )
    gt[...] = g_all[x].T
    z_send[...] = jnp.zeros_like(z_send)
    mz_send[...] = jnp.zeros_like(mz_send)
    i_send[...] = jnp.zeros_like(i_send)
    px_send[...] = jnp.zeros_like(px_send)
    count_y()
    blocks[0].core(out_block(x))
    count_z()
    acts.forward()
    blocks[0].along_y()
    load_bi.wait()
    bit[...] = bi[...].T
    count_done()
    blocks[0].along_z()
    acts.near_left()
    acts.near_right()
    acts.far()
    grads.open()

    kmc, kmy, kmz = fresh(), [fresh() for _ in range(3)], [fresh() for _ in range(7)]

    def cross(h):
        return dot(a_all[pl.ds(2 * h, 2)].reshape(2 * WA, FR), g_all[x])

    mc_send[...] = cross(1 - c).astype(BF16)
    send(mc_send, mc_recv, peer(dc=1), kmc)
    m_keep[...] = cross(c)
    blocks[4].core(in_block)
    landed(mc_recv, kmc)
    total = m_keep[...] + mc_recv[...].astype(F32)
    m_keep[...] = total
    my_send[...] = total.astype(BF16)
    for i in range(3):
        to = (y + i + 1) % 4
        send(
            my_send.at[pl.ds(pl.multiple_of(to * 160, 16), 160)],
            my_recv.at[i], peer(dy=i + 1), kmy[i],
        )
    hand_out(0, x)
    blocks[4].along_y()
    grads.forward()
    total = m_keep[pl.ds(pl.multiple_of(y * 160, 16), 160)]
    for i in range(3):
        landed(my_recv.at[i], kmy[i])
        total = total + my_recv[i].astype(F32)
    for i in range(8):
        mz_send[i, :20] = total[20 * i : 20 * i + 20].astype(BF16)
    for i in range(7):
        send(mz_send.at[(z + i + 1) % 8], mz_recv.at[i], peer(dz=i + 1), kmz[i])
    blocks[4].along_z()
    total = mz_send[z].astype(F32)
    for i in range(7):
        landed(mz_recv.at[i], kmz[i])
        total = total + mz_recv[i].astype(F32)

    kmx = [fresh() for _ in range(3)]
    mx[x] = total.astype(BF16)
    for i in range(3):
        send(mx.at[x], mx.at[x], peer(dx=i + 1), kmx[i])
    hand_in()
    load_bo.wait()
    for i in range(3):
        landed(mx.at[(x + 3 - i) % 4], kmx[i])
    total = jnp.zeros((32, WG), F32)
    for i in range(4):
        total = total + dot(mx[i], bo[i * WG : (i + 1) * WG])
    kwz, kwy, kwc = [fresh() for _ in range(7)], [fresh() for _ in range(3)], fresh()
    wz[z] = total.astype(BF16)
    for i in range(7):
        send(wz.at[z], wz.at[z], peer(dz=i + 1), kwz[i])

    grads.near_left()
    blocks[1].core(out_block(left))
    for i in range(7):
        landed(wz.at[(z + 7 - i) % 8], kwz[i])
    for i in range(8):
        wy[y, 20 * i : 20 * i + 20] = wz[i, :20]
    for i in range(3):
        send(wy.at[y], wy.at[y], peer(dy=i + 1), kwy[i])
    blocks[1].along_y()
    grads.near_right()
    blocks[2].core(out_block(right))
    for i in range(3):
        landed(wy.at[(y + 3 - i) % 4], kwy[i])
    wc[c] = wy[...].reshape(640, WG)
    send(wc.at[c], wc.at[c], peer(dc=1), kwc)
    blocks[1].along_z()
    blocks[2].along_y()
    landed(wc.at[1 - c], kwc)

    frames = n_total[:1, :1]

    def rotate(t, carry):
        rows = pl.ds(pl.multiple_of(t * 320, 16), 320)
        rotated = dot(bit[rows], wc[...].reshape(2 * 640, WG)) / frames
        st[rows] = (rotated / (ei_ref[rows] * eo_ref[...] + damping)).astype(BF16)
        return carry

    lax.fori_loop(0, 4, rotate, 0)

    def back(t, carry):
        rows = pl.ds(pl.multiple_of(t * 320, 16), 320)
        bt[rows] = dot(bi[rows], st[...]).astype(BF16)
        return carry

    lax.fori_loop(0, 4, back, 0)
    odd = group % 2
    rows = bo[pl.ds(pl.multiple_of(group * 40 - 8 * odd, 16), 48)]
    share = dot_nt(rows, bt[...])
    share = jnp.where(odd == 1, share[8:48], share[:40])
    for i in range(4):
        px_send[i, :10] = share[10 * i : 10 * i + 10].astype(BF16)
    kpx = [fresh() for _ in range(3)]
    for i in range(3):
        send(px_send.at[(x + i + 1) % 4], px_recv.at[i], peer(dx=i + 1), kpx[i])
    blocks[2].along_z()
    hand_out(1, left)
    hand_out(2, right)

    grads.far()
    blocks[3].core(out_block(opposite))
    blocks[3].along_y()
    total = px_send[x].astype(F32)
    for i in range(3):
        landed(px_recv.at[i], kpx[i])
        total = total + px_recv[i].astype(F32)
    pre_ref[...] = total[:10].astype(BF16)
    blocks[3].along_z()

    for h in range(2):

        @pl.when(jnp.logical_not(same(in_src[h])))
        def _(h=h):
            landed(i_recv.at[h], ki[h])

        cols = slice(640 * h, 640 * h + 640)
        fin_ref[:, cols] = factor_decay * prev_in_ref[:, cols] + (1.0 - factor_decay) * (
            i_recv[h, :5] / frames
        )
    hand_out(3, opposite)
    source = unit // 64
    for i, step in enumerate((0, 3, 1, 2)):

        @pl.when(jnp.logical_not(same(out_src)))
        def _(i=i):
            landed(o_recv.at[i], ko[i])

        cols = pl.ds(pl.multiple_of(((source + step) % 4) * WG, 128), WG)
        fout_ref[:, cols] = factor_decay * prev_out_ref[:, cols] + (1.0 - factor_decay) * (
            o_recv[i, :10] / frames
        )

    for copy in started:
        copy.wait_send()
    for i in range(4):

        @pl.when(jnp.logical_not(same(out_dst)))
        def _(i=i):
            out_copy(i).wait_send()

    for h in range(2):

        @pl.when(jnp.logical_not(same(in_dst[h])))
        def _(h=h):
            in_copy(h).wait_send()

    assert count[0] <= MESSAGES


def shards(
    activations, gradients, valid_frames, basis_in, basis_out, eigen_in, eigen_out,
    previous_in, previous_out,
):
    x = lax.axis_index("factor")
    eigen_rows = lax.dynamic_slice_in_dim(eigen_out, x * WG, WG, 0).reshape(1, WG)
    vmem = pl.BlockSpec(memory_space=pltpu.VMEM)
    hbm = pl.BlockSpec(memory_space=pl.ANY)
    V = pltpu.VMEM
    return pl.pallas_call(
        kernel,
        out_shape=(
            jax.ShapeDtypeStruct(previous_in.shape, F32),
            jax.ShapeDtypeStruct(previous_out.shape, F32),
            jax.ShapeDtypeStruct((10, 1280), BF16),
        ),
        in_specs=[vmem, vmem, vmem, hbm, hbm, vmem, vmem, vmem, vmem],
        out_specs=(vmem, vmem, vmem),
        scratch_shapes=[
            V((4, WA, FR), BF16), V((4, FR, WG), BF16), V((WG, FR), BF16),
            V((1280, 1280), BF16), V((2560, WG), BF16), V((1280, 1280), BF16),
            V((5, 320, 640), F32), V((5, 320, 640), BF16), V((5, 320, 640), BF16),
            V((5, 320, 640), BF16), V((5, 3, 80, 640), BF16),
            V((5, 8, 16, 640), BF16), V((5, 7, 16, 640), BF16),
            V((4, 16, 640), F32), V((4, 16, 640), F32),
            V((2, 8, 640), F32), V((2, 8, 640), F32),
            V((640, 640), F32), V((640, 640), BF16), V((640, 640), BF16),
            V((640, 640), BF16), V((3, 160, 640), BF16),
            V((8, 32, 640), BF16), V((7, 32, 640), BF16),
            V((4, 32, 640), BF16), V((8, 32, 640), BF16), V((4, 160, 640), BF16),
            V((2, 640, 640), BF16),
            V((1280, 640), BF16), V((1280, 640), BF16),
            V((4, 16, 1280), BF16), V((3, 16, 1280), BF16),
            V((2, 8, 128), F32), V((4, 8, 128), F32), V((8, 8, 128), F32),
            V((8, 128), F32),
            pltpu.SemaphoreType.DMA((MESSAGES,)), pltpu.SemaphoreType.DMA((MESSAGES,)),
            pltpu.SemaphoreType.DMA((2,)),
        ],
        compiler_params=pltpu.CompilerParams(
            collective_id=0, has_side_effects=True, vmem_limit_bytes=60 * 1024 * 1024
        ),
    )(
        activations.T, gradients, valid_frames.reshape(8, 128), basis_in, basis_out,
        eigen_rows, eigen_in.reshape(1280, 1), previous_in, previous_out,
    )


def solution(mesh):
    rows = P(("tm", "dp", "factor"), None)
    in_specs = (
        P(("tm", "dp"), "factor"),
        P(("tm", "dp"), "factor"),
        P(("tm", "dp")),
        P(),
        P(None, "factor"),
        P(),
        P(),
        rows,
        rows,
    )
    return jax.shard_map(
        shards, mesh=mesh, in_specs=in_specs, out_specs=(rows, rows, rows), check_vma=False
    )
```

```python
import functools

import jax
import jax.numpy as jnp
from jax import lax
from jax.experimental import pallas as pl
from jax.experimental.pallas import tpu as pltpu
from jax.sharding import PartitionSpec as P

factor_decay = 0.5
damping = 0.001
MESH = pl.DeviceIdType.MESH
F32 = jnp.float32
BF16 = jnp.bfloat16

FR = 1024
WA = 320
WG = 640
MESSAGES = 128


def device(x, y, z, c):
    return {"tm": y * 4 + (z % 2) * 2 + c, "dp": z // 2, "factor": x}


def dot(left, right):
    return jnp.dot(left, right, preferred_element_type=F32)


def dot_nt(left, right):
    return lax.dot_general(left, right, (((1,), (1,)), ((), ())), preferred_element_type=F32)


def kernel(
    at_ref, g_ref, valid_ref, bi_ref, bo_ref, eo_ref, ei_ref, prev_in_ref, prev_out_ref,
    fin_ref, fout_ref, pre_ref,
    a_all, g_all, gt, bi, bo, bit,
    keep, c_send, c_recv, y_send, y_recv, z_send, z_recv, o_send, o_recv, i_send, i_recv,
    ar_part, ar, bp, m_keep, mc_send, mc_recv, my_send, my_recv, mz_send, mz_recv, mx,
    qx_send, qx_recv, qz_send, qz, qy, qc,
    n_c, n_y, n_z, n_total,
    send_sem, recv_sem, load_sem,
):
    tm, dp, x = lax.axis_index("tm"), lax.axis_index("dp"), lax.axis_index("factor")
    y, c = tm // 4, tm % 2
    z = dp * 2 + (tm // 2) % 2
    group = tm * 4 + dp
    unit = group * 4 + x
    left, right, opposite = (x + 3) % 4, (x + 1) % 4, (x + 2) % 4

    def peer(dx=0, dy=0, dz=0, dc=0):
        return device((x + dx) % 4, (y + dy) % 4, (z + dz) % 8, (c + dc) % 2)

    out_unit = 64 * x + 32 * c + 8 * y + z
    out_dst = {"tm": out_unit // 16, "dp": (out_unit // 4) % 4, "factor": out_unit % 4}
    out_src = device(unit // 64, (unit // 8) % 4, unit % 8, (unit // 32) % 2)
    in_unit = [64 * x + 16 * y + 2 * z + h for h in range(2)]
    in_dst = [{"tm": u // 16, "dp": (u // 4) % 4, "factor": u % 4} for u in in_unit]
    in_src = [device(unit // 64, (unit // 16) % 4, (unit // 2) % 8, h) for h in range(2)]

    def same(d):
        return (d["tm"] == tm) & (d["dp"] == dp) & (d["factor"] == x)

    load_bi = pltpu.make_async_copy(bi_ref, bi, load_sem.at[0])
    load_bo = pltpu.make_async_copy(bo_ref, bo, load_sem.at[1])
    load_bi.start()
    load_bo.start()

    barrier = pltpu.get_barrier_semaphore()
    peers = [peer(dx=i) for i in (1, 2, 3)] + [peer(dy=i) for i in (1, 2, 3)]
    peers += [peer(dz=i) for i in range(1, 8)] + [peer(dc=1)]
    for d in peers:
        pl.semaphore_signal(barrier, inc=1, device_id=d, device_id_type=MESH)
    for d in [out_src] + in_src:

        @pl.when(jnp.logical_not(same(d)))
        def _():
            pl.semaphore_signal(barrier, inc=1, device_id=d, device_id_type=MESH)

    expected = len(peers)
    for d in [out_dst] + in_dst:
        expected = expected + jnp.where(same(d), 0, 1)

    length = jnp.sum(valid_ref[...], keepdims=True)
    a_all[x] = jnp.where(
        lax.broadcasted_iota(jnp.int32, (WA, FR), 1) < length, at_ref[...], jnp.zeros((), BF16)
    )
    n_c[0] = jnp.broadcast_to(length.astype(F32), (8, 128))
    pl.semaphore_wait(barrier, expected)

    count = [0]
    started = []

    def fresh():
        count[0] += 1
        return count[0] - 1

    def send(src, dst, to, k):
        copy = pltpu.make_async_remote_copy(
            src_ref=src, dst_ref=dst, send_sem=send_sem.at[k], recv_sem=recv_sem.at[k],
            device_id=to, device_id_type=MESH,
        )
        copy.start()
        started.append(copy)

    def landed(dst, k):
        pltpu.make_async_remote_copy(
            src_ref=dst, dst_ref=dst, send_sem=send_sem.at[k], recv_sem=recv_sem.at[k],
            device_id=peer(dx=1), device_id_type=MESH,
        ).wait_recv()

    def part(buf, shard, h, cols=None):
        rows = buf.shape[1] // 2
        if cols is None:
            return buf.at[shard, pl.ds(h * rows, rows)]
        return buf.at[shard, pl.ds(h * rows, rows), cols]

    ka = [fresh() for _ in range(6)]
    kg = [fresh() for _ in range(8)]
    near_cols, last_cols = slice(0, 384), slice(384, 640)

    def first(buf, k):
        send(part(buf, x, 0), part(buf, x, 0), peer(dx=1), k[0])
        send(part(buf, x, 1), part(buf, x, 1), peer(dx=3), k[1])

    def second(buf, k):
        send(part(buf, x, 1), part(buf, x, 1), peer(dx=1), k[2])
        send(part(buf, x, 0), part(buf, x, 0), peer(dx=3), k[3])

    def first_landed(buf, k):
        landed(part(buf, left, 0), k[0])
        landed(part(buf, right, 1), k[1])

    def second_landed(buf, k):
        landed(part(buf, left, 1), k[2])
        landed(part(buf, right, 0), k[3])

    def onward(buf, k, cols=None):
        send(part(buf, left, 0, cols), part(buf, left, 0, cols), peer(dx=1), k[0])
        send(part(buf, right, 1, cols), part(buf, right, 1, cols), peer(dx=3), k[1])

    def far_landed(buf, k, cols=None):
        landed(part(buf, opposite, 0, cols), k[0])
        landed(part(buf, opposite, 1, cols), k[1])

    first(a_all, ka)
    second(a_all, ka)

    kc, ky, kz = fresh(), [fresh() for _ in range(3)], [fresh() for _ in range(7)]
    send(n_c.at[0], n_c.at[1], peer(dc=1), kc)

    def count_y():
        landed(n_c.at[1], kc)
        n_y[0] = n_c[0] + n_c[1]
        for i in range(3):
            send(n_y.at[0], n_y.at[i + 1], peer(dy=i + 1), ky[i])

    def count_z():
        for i in range(3):
            landed(n_y.at[i + 1], ky[i])
        n_z[0] = n_y[0] + n_y[1] + n_y[2] + n_y[3]
        for i in range(7):
            send(n_z.at[0], n_z.at[i + 1], peer(dz=i + 1), kz[i])

    def count_done():
        for i in range(7):
            landed(n_z.at[i + 1], kz[i])
        total = n_z[0]
        for i in range(7):
            total = total + n_z[i + 1]
        n_total[...] = total

    class Scatter:
        def __init__(self, b, cols):
            self.b, self.cols = b, cols
            self.kc = fresh()
            self.ky = [fresh() for _ in range(3)]
            self.kz = [fresh() for _ in range(7)]

        def core(self, half):
            b, w = self.b, self.cols
            c_send[b, :, w] = half(1 - c).astype(BF16)
            send(c_send.at[b, :, w], c_recv.at[b, :, w], peer(dc=1), self.kc)
            keep[b, :, w] = half(c)

        def along_y(self):
            b, w = self.b, self.cols
            landed(c_recv.at[b, :, w], self.kc)
            total = keep[b, :, w] + c_recv[b, :, w].astype(F32)
            keep[b, :, w] = total
            y_send[b, :, w] = total.astype(BF16)
            for i in range(3):
                to = (y + i + 1) % 4
                send(
                    y_send.at[b, pl.ds(pl.multiple_of(to * 80, 16), 80), w],
                    y_recv.at[b, i, :, w], peer(dy=i + 1), self.ky[i],
                )

        def along_z(self):
            b, w = self.b, self.cols
            total = keep[b, pl.ds(pl.multiple_of(y * 80, 16), 80), w]
            for i in range(3):
                landed(y_recv.at[b, i, :, w], self.ky[i])
                total = total + y_recv[b, i, :, w].astype(F32)
            for i in range(8):
                z_send[b, i, :10, w] = total[10 * i : 10 * i + 10].astype(BF16)
            for i in range(7):
                send(
                    z_send.at[b, (z + i + 1) % 8, :, w], z_recv.at[b, i, :, w],
                    peer(dz=i + 1), self.kz[i],
                )

        def done(self):
            b, w = self.b, self.cols
            total = z_send[b, z, :, w].astype(F32)
            for i in range(7):
                landed(z_recv.at[b, i, :, w], self.kz[i])
                total = total + z_recv[b, i, :, w].astype(F32)
            return total

    whole = slice(0, 640)
    own_rows, left_rows, right_rows = (Scatter(i, whole) for i in range(3))
    far_rows, last_rows = Scatter(3, near_cols), Scatter(3, last_cols)
    in_rows = Scatter(4, whole)
    out_rows = [own_rows, left_rows, right_rows, far_rows, last_rows]
    ko = [fresh() for _ in out_rows]
    ki_send = [fresh() for _ in range(2)]
    ki = [fresh() for _ in range(2)]

    def out_place(buf, i):
        return buf.at[out_rows[i].b, :, out_rows[i].cols]

    def out_copy(i):
        return pltpu.make_async_remote_copy(
            src_ref=out_place(o_send, i), dst_ref=out_place(o_recv, i),
            send_sem=send_sem.at[ko[i]], recv_sem=recv_sem.at[ko[i]],
            device_id=out_dst, device_id_type=MESH,
        )

    def hand_out(i):
        out_place(o_send, i)[...] = out_rows[i].done()
        self_dst = same(out_dst)

        @pl.when(self_dst)
        def _():
            out_place(o_recv, i)[...] = out_place(o_send, i)[...]

        @pl.when(jnp.logical_not(self_dst))
        def _():
            out_copy(i).start()

    def in_copy(h):
        return pltpu.make_async_remote_copy(
            src_ref=i_send.at[h], dst_ref=i_recv.at[c], send_sem=send_sem.at[ki_send[h]],
            recv_sem=recv_sem.at[ki[0] + c], device_id=in_dst[h], device_id_type=MESH,
        )

    def hand_in():
        total = in_rows.done()
        for h in range(2):
            i_send[h, :5] = total[5 * h : 5 * h + 5]
        for h in range(2):
            self_dst = same(in_dst[h])

            @pl.when(self_dst)
            def _(h=h):
                i_recv[c] = i_send[h]

            @pl.when(jnp.logical_not(self_dst))
            def _(h=h):
                in_copy(h).start()

    def out_block(shard, cols):
        def half(h):
            rows = gt[pl.ds(pl.multiple_of(h * 320, 16), 320)]
            return dot(rows, g_all[shard, :, cols])

        return half

    def in_block(h):
        other = a_all[pl.ds(2 * h, 2)].reshape(2 * WA, FR)
        return dot_nt(a_all[x], other)

    g_all[x] = jnp.where(
        lax.broadcasted_iota(jnp.int32, (FR, WG), 0) < length, g_ref[...], jnp.zeros((), BF16)
    )
    gt[...] = g_all[x].T
    count_y()
    own_rows.core(out_block(x, whole))
    z_send[...] = jnp.zeros_like(z_send)
    mz_send[...] = jnp.zeros_like(mz_send)
    i_send[...] = jnp.zeros_like(i_send)
    count_z()
    first_landed(a_all, ka)
    onward(a_all, ka[4:6])
    first(g_all, kg)
    own_rows.along_y()
    load_bi.wait()
    for i in range(4):
        bit[i] = bi[i * WA : (i + 1) * WA].T
    count_done()
    own_rows.along_z()
    second_landed(a_all, ka)

    def rotate_near(t, carry):
        rows = pl.ds(pl.multiple_of(t * 320, 16), 320)
        total = dot(bit[x, rows], a_all[x]) + dot(bit[left, rows], a_all[left])
        ar_part[rows] = total + dot(bit[right, rows], a_all[right])
        return carry

    lax.fori_loop(0, 4, rotate_near, 0)
    far_landed(a_all, ka[4:6])

    def cross(h):
        def rotate_far(t, carry):
            rows = pl.ds(pl.multiple_of(h * 640 + t * 320, 16), 320)
            ar[rows] = (ar_part[rows] + dot(bit[opposite, rows], a_all[opposite])).astype(BF16)
            return carry

        lax.fori_loop(0, 2, rotate_far, 0)
        return dot(ar[pl.ds(pl.multiple_of(h * 640, 16), 640)], g_all[x])

    kmc, kmy, kmz = fresh(), [fresh() for _ in range(3)], [fresh() for _ in range(7)]
    mc_send[...] = cross(1 - c).astype(BF16)
    send(mc_send, mc_recv, peer(dc=1), kmc)
    m_keep[...] = cross(c)
    second(g_all, kg)
    landed(mc_recv, kmc)
    total = m_keep[...] + mc_recv[...].astype(F32)
    m_keep[...] = total
    my_send[...] = total.astype(BF16)
    for i in range(3):
        to = (y + i + 1) % 4
        send(
            my_send.at[pl.ds(pl.multiple_of(to * 160, 16), 160)],
            my_recv.at[i], peer(dy=i + 1), kmy[i],
        )
    in_rows.core(in_block)
    hand_out(0)

    load_bo.wait()

    def arrange(t, carry):
        to, block = t // 4, t % 4
        line = lax.broadcasted_iota(jnp.int32, (256, WG), 0)
        slot = line % 32
        at_z, second_core = line // 32, jnp.where(slot >= 10, 1, 0)
        source = (at_z % 2) * 320 + (at_z // 2) * 40 + second_core * 150 + slot + to * 10
        chosen = (lax.broadcasted_iota(jnp.int32, (256, WG), 1) == source) & (slot < 20)
        picked = dot(
            chosen.astype(F32).astype(BF16), bo[pl.ds(pl.multiple_of(block * WG, 16), WG)]
        ).astype(BF16)
        for i in range(8):
            rows = pl.ds(pl.multiple_of(i * 128 + block * 32, 32), 32)
            bp[to, rows] = picked[32 * i : 32 * i + 32]
        return carry

    lax.fori_loop(0, 16, arrange, 0)
    total = m_keep[pl.ds(pl.multiple_of(y * 160, 16), 160)]
    for i in range(3):
        landed(my_recv.at[i], kmy[i])
        total = total + my_recv[i].astype(F32)
    for i in range(8):
        mz_send[i, :20] = total[20 * i : 20 * i + 20].astype(BF16)
    for i in range(7):
        send(mz_send.at[(z + i + 1) % 8], mz_recv.at[i], peer(dz=i + 1), kmz[i])
    in_rows.along_y()
    first_landed(g_all, kg)
    total = mz_send[z].astype(F32)
    for i in range(7):
        landed(mz_recv.at[i], kmz[i])
        total = total + mz_recv[i].astype(F32)

    kmx = [fresh() for _ in range(3)]
    mx[x] = total.astype(BF16)
    for i in range(3):
        send(mx.at[x], mx.at[x], peer(dx=i + 1), kmx[i])
    onward(g_all, kg[4:6], near_cols)
    in_rows.along_z()
    frames = n_total[:1, :1]
    row = lax.broadcasted_iota(jnp.int32, (32, 1280), 0) + (c * 640 + y * 160 + z * 20)
    here = lax.broadcasted_iota(jnp.int32, (32, 1280), 1) == row
    eigen_rows = jnp.concatenate([ei_ref[i : i + 1] for i in range(10)], axis=1)
    eigen_rows = jnp.sum(jnp.where(here, eigen_rows, 0.0), axis=1, keepdims=True)
    eigen_cols = jnp.concatenate([eo_ref[pl.ds(5 * x + i, 1)] for i in range(5)], axis=1)
    for i in range(3):
        landed(mx.at[(x + 3 - i) % 4], kmx[i])
    total = jnp.zeros((32, WG), F32)
    for i in range(4):
        total = total + dot(mx[i], bo[i * WG : (i + 1) * WG])
    scaled = (total / frames / (eigen_rows * eigen_cols + damping)).astype(BF16)
    kqx, kqz = [fresh() for _ in range(3)], [fresh() for _ in range(7)]
    kqy, kqc = [fresh() for _ in range(3)], fresh()
    for i in range(4):
        qx_send[i] = dot_nt(scaled, bp[i]).astype(BF16)
    for i in range(3):
        send(qx_send.at[(x + i + 1) % 4], qx_recv.at[i], peer(dx=i + 1), kqx[i])
    onward(g_all, kg[6:8], last_cols)
    second_landed(g_all, kg)
    left_rows.core(out_block(left, whole))
    hand_in()
    total = qx_send[x].astype(F32)
    for i in range(3):
        landed(qx_recv.at[i], kqx[i])
        total = total + qx_recv[i].astype(F32)
    for i in range(8):
        qz_send[i] = total[:, 128 * i : 128 * i + 128].astype(BF16)
    qz[z] = qz_send[z]
    for i in range(7):
        send(qz_send.at[(z + i + 1) % 8], qz.at[z], peer(dz=i + 1), kqz[i])
    left_rows.along_y()
    right_rows.core(out_block(right, whole))
    for i in range(7):
        landed(qz.at[(z + 7 - i) % 8], kqz[i])
    for i in range(8):
        qy[y, 20 * i : 20 * i + 20] = qz[i, :20]
    for i in range(3):
        send(qy.at[y], qy.at[y], peer(dy=i + 1), kqy[i])
    right_rows.along_y()
    left_rows.along_z()
    for i in range(3):
        landed(qy.at[(y + 3 - i) % 4], kqy[i])
    qc[c] = qy[...].reshape(640, 128)
    send(qc.at[c], qc.at[c], peer(dc=1), kqc)
    far_landed(g_all, kg[4:6], near_cols)
    far_rows.core(out_block(opposite, near_cols))
    right_rows.along_z()
    far_rows.along_y()
    landed(qc.at[1 - c], kqc)
    mine = lax.broadcasted_iota(jnp.int32, (16, 128), 0) + (y * 32 + c * 10)
    mine = lax.broadcasted_iota(jnp.int32, (16, 128), 1) == mine
    picked = dot_nt(mine.astype(F32).astype(BF16), qc[...].reshape(1280, 128)).astype(BF16)
    pre_ref[...] = dot_nt(picked, bi[...])[:10].astype(BF16)
    hand_out(1)

    far_landed(g_all, kg[6:8], last_cols)
    last_rows.core(out_block(opposite, last_cols))
    far_rows.along_z()
    last_rows.along_y()
    hand_out(2)
    last_rows.along_z()
    hand_out(3)

    for h in range(2):

        @pl.when(jnp.logical_not(same(in_src[h])))
        def _(h=h):
            landed(i_recv.at[h], ki[h])

        cols = slice(640 * h, 640 * h + 640)
        fin_ref[:, cols] = factor_decay * prev_in_ref[:, cols] + (1.0 - factor_decay) * (
            i_recv[h, :5] / frames
        )
    hand_out(4)
    source = unit // 64
    for i, step in enumerate((0, 3, 1, 2, 2)):

        @pl.when(jnp.logical_not(same(out_src)))
        def _(i=i):
            landed(out_place(o_recv, i), ko[i])

        w = out_rows[i].cols
        cols = pl.ds(pl.multiple_of(((source + step) % 4) * WG, 128) + w.start, w.stop - w.start)
        fout_ref[:, cols] = factor_decay * prev_out_ref[:, cols] + (1.0 - factor_decay) * (
            o_recv[out_rows[i].b, :10, w] / frames
        )

    for copy in started:
        copy.wait_send()
    for i in range(5):

        @pl.when(jnp.logical_not(same(out_dst)))
        def _(i=i):
            out_copy(i).wait_send()

    for h in range(2):

        @pl.when(jnp.logical_not(same(in_dst[h])))
        def _(h=h):
            in_copy(h).wait_send()

    assert count[0] <= MESSAGES


def shards(
    activations, gradients, valid_frames, basis_in, basis_out, eigen_in, eigen_out,
    previous_in, previous_out,
):
    vmem = pl.BlockSpec(memory_space=pltpu.VMEM)
    hbm = pl.BlockSpec(memory_space=pl.ANY)
    V = pltpu.VMEM
    return pl.pallas_call(
        kernel,
        out_shape=(
            jax.ShapeDtypeStruct(previous_in.shape, F32),
            jax.ShapeDtypeStruct(previous_out.shape, F32),
            jax.ShapeDtypeStruct((10, 1280), BF16),
        ),
        in_specs=[vmem, vmem, vmem, hbm, hbm, vmem, vmem, vmem, vmem],
        out_specs=(vmem, vmem, vmem),
        scratch_shapes=[
            V((4, WA, FR), BF16), V((4, FR, WG), BF16), V((WG, FR), BF16),
            V((1280, 1280), BF16), V((2560, WG), BF16), V((4, 1280, WA), BF16),
            V((5, 320, 640), F32), V((5, 320, 640), BF16), V((5, 320, 640), BF16),
            V((5, 320, 640), BF16), V((5, 3, 80, 640), BF16),
            V((5, 8, 16, 640), BF16), V((5, 7, 16, 640), BF16),
            V((4, 16, 640), F32), V((4, 16, 640), F32),
            V((2, 8, 640), F32), V((2, 8, 640), F32),
            V((1280, FR), F32), V((1280, FR), BF16), V((4, 1024, WG), BF16),
            V((640, 640), F32), V((640, 640), BF16), V((640, 640), BF16),
            V((640, 640), BF16), V((3, 160, 640), BF16),
            V((8, 32, 640), BF16), V((7, 32, 640), BF16),
            V((4, 32, 640), BF16),
            V((4, 32, 1024), BF16), V((3, 32, 1024), BF16), V((8, 32, 128), BF16),
            V((8, 32, 128), BF16), V((4, 160, 128), BF16), V((2, 640, 128), BF16),
            V((2, 8, 128), F32), V((4, 8, 128), F32), V((8, 8, 128), F32),
            V((8, 128), F32),
            pltpu.SemaphoreType.DMA((MESSAGES,)), pltpu.SemaphoreType.DMA((MESSAGES,)),
            pltpu.SemaphoreType.DMA((2,)),
        ],
        compiler_params=pltpu.CompilerParams(
            collective_id=0, has_side_effects=True, vmem_limit_bytes=60 * 1024 * 1024
        ),
    )(
        activations.T, gradients, valid_frames.reshape(8, 128), basis_in, basis_out,
        eigen_out.reshape(20, 128), eigen_in.reshape(10, 128), previous_in, previous_out,
    )


def solution(mesh):
    rows = P(("tm", "dp", "factor"), None)
    in_specs = (
        P(("tm", "dp"), "factor"),
        P(("tm", "dp"), "factor"),
        P(("tm", "dp")),
        P(),
        P(None, "factor"),
        P(),
        P(),
        rows,
        rows,
    )
    return jax.shard_map(
        shards, mesh=mesh, in_specs=in_specs, out_specs=(rows, rows, rows), check_vma=False
    )
```

```python
import functools

import jax
import jax.numpy as jnp
from jax import lax
from jax.experimental import pallas as pl
from jax.experimental.pallas import tpu as pltpu
from jax.sharding import PartitionSpec as P

factor_decay = 0.5
damping = 0.001
MESH = pl.DeviceIdType.MESH
F32 = jnp.float32
BF16 = jnp.bfloat16

FR = 1024
WA = 320
WG = 640
MESSAGES = 144


def device(x, y, z, c):
    return {"tm": y * 4 + (z % 2) * 2 + c, "dp": z // 2, "factor": x}


def dot(left, right):
    return jnp.dot(left, right, preferred_element_type=F32)


def dot_nt(left, right):
    return lax.dot_general(left, right, (((1,), (1,)), ((), ())), preferred_element_type=F32)


WIDTHS = (640, 640, 768, 512, 384, 256)


def lines_of(width):
    return (10 * (width // 128) + 15) // 16 * 16


def kernel(
    at_ref, g_ref, valid_ref, bi_ref, bo_ref, eo_ref, ei_ref, prev_in_ref, prev_out_ref,
    fin_ref, fout_ref, pre_ref,
    a_all, g_all, gt, bi, bo, bit,
    keeps, c_sends, c_recvs, y_sends, y_recvs, z_sends, z_recvs, o_sends, o_recvs, i_send, i_recv,
    ar_part, ar, chosen, g_raw, m_keep, mc_send, mc_recv, my_send, my_recv, mz_send, mz_recv, mx,
    qx_send, qx_recv, qz_send, qz, qy, qc,
    n_c, n_y, n_z, n_total,
    send_sem, recv_sem, load_sem,
):
    tm, dp, x = lax.axis_index("tm"), lax.axis_index("dp"), lax.axis_index("factor")
    y, c = tm // 4, tm % 2
    z = dp * 2 + (tm // 2) % 2
    group = tm * 4 + dp
    unit = group * 4 + x
    left, right, opposite = (x + 3) % 4, (x + 1) % 4, (x + 2) % 4

    def peer(dx=0, dy=0, dz=0, dc=0):
        return device((x + dx) % 4, (y + dy) % 4, (z + dz) % 8, (c + dc) % 2)

    turn_dsts = [device(i, x, z, c) for i in range(4)]
    turn_srcs = [device(y, i, z, c) for i in range(4)]
    own_unit = 64 * x + 32 * c + 8 * y + z
    out_dst = {"tm": own_unit // 16, "dp": (own_unit // 4) % 4, "factor": own_unit % 4}
    out_src = device(unit // 64, (unit // 8) % 4, unit % 8, (unit // 32) % 2)
    in_unit = [64 * x + 16 * y + 2 * z + h for h in range(2)]
    in_dst = [{"tm": u // 16, "dp": (u // 4) % 4, "factor": u % 4} for u in in_unit]
    in_src = [device(unit // 64, (unit // 16) % 4, (unit // 2) % 8, h) for h in range(2)]

    def same(d):
        return (d["tm"] == tm) & (d["dp"] == dp) & (d["factor"] == x)

    load_bi = pltpu.make_async_copy(bi_ref, bi, load_sem.at[0])
    load_bo = pltpu.make_async_copy(bo_ref, bo, load_sem.at[1])
    load_g = pltpu.make_async_copy(g_ref, g_raw, load_sem.at[2])
    load_g.start()
    load_bi.start()
    load_bo.start()

    barrier = pltpu.get_barrier_semaphore()
    peers = [peer(dx=i) for i in (1, 2, 3)] + [peer(dy=i) for i in (1, 2, 3)]
    peers += [peer(dz=i) for i in range(1, 8)] + [peer(dc=1)]
    for d in peers:
        pl.semaphore_signal(barrier, inc=1, device_id=d, device_id_type=MESH)
    for d in turn_srcs + [out_src] + in_src:

        @pl.when(jnp.logical_not(same(d)))
        def _():
            pl.semaphore_signal(barrier, inc=1, device_id=d, device_id_type=MESH)

    expected = len(peers)
    for d in turn_dsts + [out_dst] + in_dst:
        expected = expected + jnp.where(same(d), 0, 1)

    length = jnp.sum(valid_ref[...], keepdims=True)
    a_all[x] = jnp.where(
        lax.broadcasted_iota(jnp.int32, (WA, FR), 1) < length, at_ref[...], jnp.zeros((), BF16)
    )
    n_c[0] = jnp.broadcast_to(length.astype(F32), (8, 128))
    mx[x] = jnp.zeros((32, WG), BF16)
    qz_send[...] = jnp.zeros_like(qz_send)
    pl.semaphore_wait(barrier, expected)

    count = [0]
    started = []

    def fresh():
        count[0] += 1
        return count[0] - 1

    def send(src, dst, to, k):
        copy = pltpu.make_async_remote_copy(
            src_ref=src, dst_ref=dst, send_sem=send_sem.at[k], recv_sem=recv_sem.at[k],
            device_id=to, device_id_type=MESH,
        )
        copy.start()
        started.append(copy)

    def landed(dst, k):
        pltpu.make_async_remote_copy(
            src_ref=dst, dst_ref=dst, send_sem=send_sem.at[k], recv_sem=recv_sem.at[k],
            device_id=peer(dx=1), device_id_type=MESH,
        ).wait_recv()

    def part(buf, shard, h, cols=None):
        rows = buf.shape[1] // 2
        rows = pl.ds(0, buf.shape[1]) if h is None else pl.ds(h * rows, rows)
        return buf.at[shard, rows] if cols is None else buf.at[shard, rows, cols]

    ka = [fresh() for _ in range(6)]
    kg = [fresh() for _ in range(8)]
    near_cols, last_cols = slice(0, 384), slice(384, 640)

    def both(buf, k, to_right, to_left, cols=None):
        for shard, h, i in ((x, to_right, 1), (x, to_left, 3)):
            at = part(buf, shard, h, cols)
            send(at, at, peer(dx=i), k[i // 2])

    def both_landed(buf, k, from_left, from_right, cols=None):
        landed(part(buf, left, from_left, cols), k[0])
        landed(part(buf, right, from_right, cols), k[1])

    def onward(buf, k, cols=None):
        send(part(buf, left, 0, cols), part(buf, left, 0, cols), peer(dx=1), k[0])
        send(part(buf, right, 1, cols), part(buf, right, 1, cols), peer(dx=3), k[1])

    def far_landed(buf, k, cols=None):
        landed(part(buf, opposite, 0, cols), k[0])
        landed(part(buf, opposite, 1, cols), k[1])

    both(a_all, ka[0:2], 0, 1)
    both(a_all, ka[2:4], 1, 0)

    kc, ky, kz = fresh(), [fresh() for _ in range(3)], [fresh() for _ in range(7)]
    send(n_c.at[0], n_c.at[1], peer(dc=1), kc)

    def count_y():
        landed(n_c.at[1], kc)
        n_y[0] = n_c[0] + n_c[1]
        for i in range(3):
            send(n_y.at[0], n_y.at[i + 1], peer(dy=i + 1), ky[i])

    def count_z():
        for i in range(3):
            landed(n_y.at[i + 1], ky[i])
        n_z[0] = n_y[0] + n_y[1] + n_y[2] + n_y[3]
        for i in range(7):
            send(n_z.at[0], n_z.at[i + 1], peer(dz=i + 1), kz[i])

    def count_done():
        for i in range(7):
            landed(n_z.at[i + 1], kz[i])
        total = n_z[0]
        for i in range(7):
            total = total + n_z[i + 1]
        n_total[...] = total

    class Scatter:
        def __init__(self, b):
            self.tiles = WIDTHS[b] // 128
            self.keep, self.c_send, self.c_recv = keeps[b], c_sends[b], c_recvs[b]
            self.y_send, self.y_recv = y_sends[b], y_recvs[b]
            self.z_send, self.z_recv = z_sends[b], z_recvs[b]
            self.o_send, self.o_recv = o_sends[b], o_recvs[b]
            self.kc, self.ko = fresh(), fresh()
            self.ky = [fresh() for _ in range(3)]
            self.kz = [fresh() for _ in range(7)]

        def core(self, half):
            self.c_send[...] = half(1 - c).astype(BF16)
            send(self.c_send, self.c_recv, peer(dc=1), self.kc)
            self.keep[...] = half(c)

        def along_y(self):
            landed(self.c_recv, self.kc)
            total = self.keep[...] + self.c_recv[...].astype(F32)
            self.keep[...] = total
            self.y_send[...] = total.astype(BF16)
            for i in range(3):
                to = (y + i + 1) % 4
                send(
                    self.y_send.at[pl.ds(pl.multiple_of(to * 80, 16), 80)],
                    self.y_recv.at[i], peer(dy=i + 1), self.ky[i],
                )

        def sum_y(self):
            total = self.keep[pl.ds(pl.multiple_of(y * 80, 16), 80)]
            for i in range(3):
                landed(self.y_recv.at[i], self.ky[i])
                total = total + self.y_recv[i].astype(F32)
            return total

        def along_z(self):
            total = self.sum_y()
            for i in range(8):
                pieces = [
                    total[10 * i : 10 * i + 10, 128 * j : 128 * j + 128] for j in range(self.tiles)
                ]
                pieces = jnp.concatenate(pieces, axis=0).astype(BF16)
                self.z_send[i, : 10 * self.tiles] = pieces
            for i in range(7):
                send(
                    self.z_send.at[(z + i + 1) % 8], self.z_recv.at[i],
                    peer(dz=i + 1), self.kz[i],
                )

        def done(self):
            total = self.z_send[z].astype(F32)
            for i in range(7):
                landed(self.z_recv.at[i], self.kz[i])
                total = total + self.z_recv[i].astype(F32)
            return total

        def out_copy(self):
            return pltpu.make_async_remote_copy(
                src_ref=self.o_send, dst_ref=self.o_recv, send_sem=send_sem.at[self.ko],
                recv_sem=recv_sem.at[self.ko], device_id=out_dst, device_id_type=MESH,
            )

        def hand_out(self):
            self.o_send[...] = self.done()
            self_dst = same(out_dst)

            @pl.when(self_dst)
            def _():
                self.o_recv[...] = self.o_send[...]

            @pl.when(jnp.logical_not(self_dst))
            def _():
                self.out_copy().start()

        def handed_out(self):
            @pl.when(jnp.logical_not(same(out_src)))
            def _():
                landed(self.o_recv, self.ko)

            return self.o_recv[...]

    class Turned(Scatter):
        def __init__(self, b):
            super().__init__(b)
            self.k_send, self.k = [fresh() for _ in range(4)], [fresh() for _ in range(4)]

        def copy(self, i):
            return pltpu.make_async_remote_copy(
                src_ref=self.y_send.at[pl.ds(80 * i, 80)], dst_ref=self.y_recv.at[y],
                send_sem=send_sem.at[self.k_send[i]], recv_sem=recv_sem.at[self.k[0] + y],
                device_id=turn_dsts[i], device_id_type=MESH,
            )

        def along_y(self):
            landed(self.c_recv, self.kc)
            total = self.keep[...] + self.c_recv[...].astype(F32)
            for i in range(4):
                starts = [(j % 2) * 160 + (j // 2) * 40 + 10 * i for j in range(8)]
                pieces = [total[start : start + 10] for start in starts]
                self.y_send[80 * i : 80 * i + 80] = jnp.concatenate(pieces, axis=0).astype(BF16)
            for i in range(4):
                self_dst = same(turn_dsts[i])

                @pl.when(self_dst)
                def _(i=i):
                    self.y_recv[y] = self.y_send[80 * i : 80 * i + 80]

                @pl.when(jnp.logical_not(self_dst))
                def _(i=i):
                    self.copy(i).start()

        def sum_y(self):
            total = jnp.zeros((80, 128 * self.tiles), F32)
            for i in range(4):

                @pl.when(jnp.logical_not(same(turn_srcs[i])))
                def _(i=i):
                    landed(self.y_recv.at[i], self.k[i])

                total = total + self.y_recv[i].astype(F32)
            return total

    in_rows, own_rows, near_rows, second_rows, far_rows = (Scatter(i) for i in range(5))
    last_rows = Turned(5)
    ki_send = [fresh() for _ in range(2)]
    ki = [fresh() for _ in range(2)]

    def in_copy(h):
        return pltpu.make_async_remote_copy(
            src_ref=i_send.at[h], dst_ref=i_recv.at[c], send_sem=send_sem.at[ki_send[h]],
            recv_sem=recv_sem.at[ki[0] + c], device_id=in_dst[h], device_id_type=MESH,
        )

    def hand_in():
        total = in_rows.done()
        for h in range(2):
            for j in range(5):
                lanes = slice(128 * j, 128 * j + 128)
                i_send[h, :5, lanes] = total[10 * j + 5 * h : 10 * j + 5 * h + 5]
        for h in range(2):
            self_dst = same(in_dst[h])

            @pl.when(self_dst)
            def _(h=h):
                i_recv[c] = i_send[h]

            @pl.when(jnp.logical_not(self_dst))
            def _(h=h):
                in_copy(h).start()

    def own_half(h):
        return dot(gt[pl.ds(pl.multiple_of(h * 320, 16), 320)], g_all[x])

    def near_half(cols):
        def half(h):
            rows = gt[pl.ds(pl.multiple_of(h * 320, 16), 320)]
            sides = [dot(rows, g_all[shard, :, cols]) for shard in (left, right)]
            return jnp.concatenate(sides, axis=1)

        return half

    def far_half(h):
        rows = gt[pl.ds(pl.multiple_of(h * 320, 16), 320)]
        return dot(rows, g_all[opposite, :, near_cols])

    def last_half(h):
        rows = [gt[pl.ds(pl.multiple_of(i * 320 + h * 160, 16), 160)] for i in range(2)]
        return dot(jnp.concatenate(rows, axis=0), g_all[opposite, :, last_cols])

    def in_block(h):
        other = a_all[pl.ds(2 * h, 2)].reshape(2 * WA, FR)
        return dot_nt(a_all[x], other)

    load_g.wait()
    g_all[x] = jnp.where(
        lax.broadcasted_iota(jnp.int32, (FR, WG), 0) < length, g_raw[...], jnp.zeros((), BF16)
    )
    gt[...] = g_all[x].T
    own_rows.core(own_half)
    count_y()
    for buf in z_sends:
        buf[...] = jnp.zeros_like(buf)
    mz_send[...] = jnp.zeros_like(mz_send)
    i_send[...] = jnp.zeros_like(i_send)
    own_rows.along_y()
    count_z()
    both_landed(a_all, ka[0:2], 0, 1)
    onward(a_all, ka[4:6])
    both(g_all, kg[0:2], None, None, near_cols)
    load_bi.wait()
    for i in range(4):
        bit[i] = bi[i * WA : (i + 1) * WA].T

    line = lax.broadcasted_iota(jnp.int32, (256, WG), 0)
    slot, at_z = line % 32, line // 32
    source = (at_z % 2) * 320 + (at_z // 2) * 40 + jnp.where(slot >= 10, 150, 0) + slot
    source = jnp.where(slot < 20, source, -WG)
    ahead = lax.broadcasted_iota(jnp.int32, (256, WG), 1) - source
    for i in range(4):
        chosen[i] = (ahead == 10 * i).astype(F32).astype(BF16)
    own_rows.along_z()
    count_done()
    both_landed(a_all, ka[2:4], 1, 0)

    def rotate_near(t, carry):
        rows = pl.ds(pl.multiple_of(t * 320, 16), 320)
        total = dot(bit[x, rows], a_all[x]) + dot(bit[left, rows], a_all[left])
        ar_part[rows] = total + dot(bit[right, rows], a_all[right])
        return carry

    lax.fori_loop(0, 4, rotate_near, 0)
    far_landed(a_all, ka[4:6])

    def cross(h):
        def rotate_far(t, carry):
            rows = pl.ds(pl.multiple_of(h * 640 + t * 320, 16), 320)
            ar[rows] = (ar_part[rows] + dot(bit[opposite, rows], a_all[opposite])).astype(BF16)
            return carry

        lax.fori_loop(0, 2, rotate_far, 0)
        return dot(ar[pl.ds(pl.multiple_of(h * 640, 16), 640)], g_all[x])

    kmc, kmy, kmz = fresh(), [fresh() for _ in range(3)], [fresh() for _ in range(7)]
    mc_send[...] = cross(1 - c).astype(BF16)
    send(mc_send, mc_recv, peer(dc=1), kmc)
    m_keep[...] = cross(c)
    both(g_all, kg[2:4], None, None, last_cols)
    landed(mc_recv, kmc)
    total = m_keep[...] + mc_recv[...].astype(F32)
    m_keep[...] = total
    my_send[...] = total.astype(BF16)
    for i in range(3):
        to = (y + i + 1) % 4
        send(
            my_send.at[pl.ds(pl.multiple_of(to * 160, 16), 160)],
            my_recv.at[i], peer(dy=i + 1), kmy[i],
        )
    in_rows.core(in_block)
    own_rows.hand_out()
    load_bo.wait()
    in_rows.along_y()
    total = m_keep[pl.ds(pl.multiple_of(y * 160, 16), 160)]
    for i in range(3):
        landed(my_recv.at[i], kmy[i])
        total = total + my_recv[i].astype(F32)
    for i in range(8):
        pieces = [total[20 * i : 20 * i + 20, 128 * j : 128 * j + 128] for j in range(5)]
        mz_send[i, :100] = jnp.concatenate(pieces, axis=0).astype(BF16)
    for i in range(7):
        send(mz_send.at[(z + i + 1) % 8], mz_recv.at[i], peer(dz=i + 1), kmz[i])
    both_landed(g_all, kg[0:2], None, None, near_cols)
    near_rows.core(near_half(near_cols))
    frames = n_total[:1, :1]
    row = lax.broadcasted_iota(jnp.int32, (32, 1280), 0) + (c * 640 + y * 160 + z * 20)
    here = lax.broadcasted_iota(jnp.int32, (32, 1280), 1) == row
    eigen_rows = jnp.concatenate([ei_ref[i : i + 1] for i in range(10)], axis=1)
    eigen_rows = jnp.sum(jnp.where(here, eigen_rows, 0.0), axis=1, keepdims=True)
    eigen_cols = jnp.concatenate([eo_ref[pl.ds(5 * x + i, 1)] for i in range(5)], axis=1)
    scale = eigen_rows * eigen_cols + damping
    total = mz_send[z].astype(F32)
    for i in range(7):
        landed(mz_recv.at[i], kmz[i])
        total = total + mz_recv[i].astype(F32)

    kmx = [fresh() for _ in range(3)]
    for j in range(5):
        mx[x, :20, 128 * j : 128 * j + 128] = total[20 * j : 20 * j + 20].astype(BF16)
    for i in range(3):
        send(mx.at[x], mx.at[x], peer(dx=i + 1), kmx[i])
    onward(g_all, kg[4:6], near_cols)
    in_rows.along_z()
    near_rows.along_y()
    both_landed(g_all, kg[2:4], None, None, last_cols)
    second_rows.core(near_half(last_cols))
    near_rows.along_z()
    for i in range(3):
        landed(mx.at[(x + 3 - i) % 4], kmx[i])
    total = jnp.zeros((32, WG), F32)
    for i in range(4):
        total = total + dot(mx[i], bo[i * WG : (i + 1) * WG])
    scaled = (total / frames / scale).astype(BF16)
    kqx, kqz = [fresh() for _ in range(3)], [fresh() for _ in range(7)]
    kqy, kqc = [fresh() for _ in range(3)], fresh()
    turned = dot_nt(scaled, bo[...]).astype(BF16)
    turned = jnp.concatenate([turned[:20, WG * i : WG * i + WG] for i in range(4)], axis=0)
    for i in range(4):
        qx_send[i] = dot_nt(turned, chosen[i]).astype(BF16)
    for i in range(3):
        send(qx_send.at[(x + i + 1) % 4], qx_recv.at[i], peer(dx=i + 1), kqx[i])
    onward(g_all, kg[6:8], last_cols)
    second_rows.along_y()
    hand_in()
    near_rows.hand_out()
    far_landed(g_all, kg[4:6], near_cols)
    far_rows.core(far_half)
    total = qx_send[x].astype(F32)
    for i in range(3):
        landed(qx_recv.at[i], kqx[i])
        total = total + qx_recv[i].astype(F32)
    for i in range(8):
        lanes = slice(32 * i, 32 * i + 32)
        pieces = [total[20 * j : 20 * j + 20, lanes] for j in range(4)]
        qz_send[i, :20] = jnp.concatenate(pieces, axis=1).astype(BF16)
    qz[z] = qz_send[z]
    for i in range(7):
        send(qz_send.at[(z + i + 1) % 8], qz.at[z], peer(dz=i + 1), kqz[i])
    second_rows.along_z()
    far_rows.along_y()
    for i in range(7):
        landed(qz.at[(z + 7 - i) % 8], kqz[i])
    for i in range(8):
        qy[y, 20 * i : 20 * i + 20] = qz[i, :20]
    for i in range(3):
        send(qy.at[y], qy.at[y], peer(dy=i + 1), kqy[i])

    far_landed(g_all, kg[6:8], last_cols)
    last_rows.core(last_half)
    far_rows.along_z()
    for i in range(3):
        landed(qy.at[(y + 3 - i) % 4], kqy[i])
    qc[c] = qy[...].reshape(640, 128)
    send(qc.at[c], qc.at[c], peer(dc=1), kqc)
    last_rows.along_y()
    second_rows.hand_out()
    far_rows.hand_out()
    last_rows.along_z()
    landed(qc.at[1 - c], kqc)
    mine = lax.broadcasted_iota(jnp.int32, (16, 128), 0) + (y * 32 + c * 10)
    mine = lax.broadcasted_iota(jnp.int32, (16, 128), 1) == mine
    picked = dot_nt(mine.astype(F32).astype(BF16), qc[...].reshape(1280, 128)).astype(BF16)
    pre_ref[...] = dot_nt(picked, bi[...])[:10].astype(BF16)

    for h in range(2):

        @pl.when(jnp.logical_not(same(in_src[h])))
        def _(h=h):
            landed(i_recv.at[h], ki[h])

        cols = slice(640 * h, 640 * h + 640)
        fin_ref[:, cols] = factor_decay * prev_in_ref[:, cols] + (1.0 - factor_decay) * (
            i_recv[h, :5] / frames
        )
    source = unit // 64

    def write_out(places, total):
        for j, (step, lane) in enumerate(places):
            at = pl.multiple_of(((source + step) % 4) * WG, 128) + lane
            lanes = pl.ds(pl.multiple_of(at, 128), 128)
            fout_ref[:, lanes] = factor_decay * prev_out_ref[:, lanes] + (1.0 - factor_decay) * (
                total[10 * j : 10 * j + 10] / frames
            )

    def tiles(step, cols=None):
        start, stop = (0, WG) if cols is None else (cols.start, cols.stop)
        return [(step, lane) for lane in range(start, stop, 128)]

    write_out(tiles(0), own_rows.handed_out())
    write_out(tiles(3, near_cols) + tiles(1, near_cols), near_rows.handed_out())
    write_out(tiles(3, last_cols) + tiles(1, last_cols), second_rows.handed_out())
    write_out(tiles(2, near_cols), far_rows.handed_out())
    write_out(tiles(2, last_cols), last_rows.done())

    for copy in started:
        copy.wait_send()
    @pl.when(jnp.logical_not(same(out_dst)))
    def _():
        for rows in (own_rows, near_rows, second_rows, far_rows):
            rows.out_copy().wait_send()

    for i in range(4):

        @pl.when(jnp.logical_not(same(turn_dsts[i])))
        def _(i=i):
            last_rows.copy(i).wait_send()

    for h in range(2):

        @pl.when(jnp.logical_not(same(in_dst[h])))
        def _(h=h):
            in_copy(h).wait_send()

    assert count[0] <= MESSAGES


def handed_on(*refs):
    for i in range(3):
        refs[3 + i][...] = refs[i][...]


def shards(
    activations, gradients, valid_frames, basis_in, basis_out, eigen_in, eigen_out,
    previous_in, previous_out,
):
    vmem = pl.BlockSpec(memory_space=pltpu.VMEM)
    hbm = pl.BlockSpec(memory_space=pl.ANY)
    V = pltpu.VMEM
    results = pl.pallas_call(
        kernel,
        out_shape=(
            jax.ShapeDtypeStruct(previous_in.shape, F32),
            jax.ShapeDtypeStruct(previous_out.shape, F32),
            jax.ShapeDtypeStruct((10, 1280), BF16),
        ),
        in_specs=[vmem, hbm, vmem, hbm, hbm, vmem, vmem, vmem, vmem],
        out_specs=(vmem, vmem, vmem),
        scratch_shapes=[
            V((4, WA, FR), BF16), V((4, FR, WG), BF16), V((WG, FR), BF16),
            V((1280, 1280), BF16), V((2560, WG), BF16), V((4, 1280, WA), BF16),
            [V((320, w), F32) for w in WIDTHS], [V((320, w), BF16) for w in WIDTHS],
            [V((320, w), BF16) for w in WIDTHS], [V((320, w), BF16) for w in WIDTHS],
            [V((4, 80, w), BF16) for w in WIDTHS], [V((8, lines_of(w), 128), BF16) for w in WIDTHS],
            [V((7, lines_of(w), 128), BF16) for w in WIDTHS],
            [V((lines_of(w), 128), F32) for w in WIDTHS], [V((lines_of(w), 128), F32) for w in WIDTHS],
            V((2, 8, 640), F32), V((2, 8, 640), F32),
            V((1280, FR), F32), V((1280, FR), BF16), V((4, 256, WG), BF16),
            V((FR, WG), BF16),
            V((640, 640), F32), V((640, 640), BF16), V((640, 640), BF16),
            V((640, 640), BF16), V((3, 160, 640), BF16),
            V((8, 112, 128), BF16), V((7, 112, 128), BF16),
            V((4, 32, 640), BF16),
            V((4, 80, 256), BF16), V((3, 80, 256), BF16), V((8, 32, 128), BF16),
            V((8, 32, 128), BF16), V((4, 160, 128), BF16), V((2, 640, 128), BF16),
            V((2, 8, 128), F32), V((4, 8, 128), F32), V((8, 8, 128), F32),
            V((8, 128), F32),
            pltpu.SemaphoreType.DMA((MESSAGES,)), pltpu.SemaphoreType.DMA((MESSAGES,)),
            pltpu.SemaphoreType.DMA((3,)),
        ],
        compiler_params=pltpu.CompilerParams(
            collective_id=0, has_side_effects=True, vmem_limit_bytes=60 * 1024 * 1024
        ),
    )(
        activations.T, gradients, valid_frames.reshape(8, 128), basis_in, basis_out,
        eigen_out.reshape(20, 128), eigen_in.reshape(10, 128), previous_in, previous_out,
    )
    return pl.pallas_call(
        handed_on,
        out_shape=[jax.ShapeDtypeStruct(r.shape, r.dtype) for r in results],
        in_specs=[vmem] * 3,
        out_specs=[vmem] * 3,
    )(*results)


def solution(mesh):
    rows = P(("tm", "dp", "factor"), None)
    in_specs = (
        P(("tm", "dp"), "factor"),
        P(("tm", "dp"), "factor"),
        P(("tm", "dp")),
        P(),
        P(None, "factor"),
        P(),
        P(),
        rows,
        rows,
    )
    return jax.shard_map(
        shards, mesh=mesh, in_specs=in_specs, out_specs=(rows, rows, rows), check_vma=False
    )
```

```python
import functools

import jax
import jax.numpy as jnp
from jax import lax
from jax.experimental import pallas as pl
from jax.experimental.pallas import tpu as pltpu
from jax.sharding import PartitionSpec as P

factor_decay = 0.5
damping = 0.001
MESH = pl.DeviceIdType.MESH
F32 = jnp.float32
BF16 = jnp.bfloat16

FR = 1024
WA = 320
WG = 640
MESSAGES = 80


def device(x, y, z, c):
    return {"tm": y * 4 + (z % 2) * 2 + c, "dp": z // 2, "factor": x}


def dot(left, right):
    return jnp.dot(left, right, preferred_element_type=F32)


def dot_nt(left, right):
    return lax.dot_general(left, right, (((1,), (1,)), ((), ())), preferred_element_type=F32)


WIDTHS = (640, 640, 768, 512, 384, 256)


def lines_of(width):
    return (10 * (width // 128) + 15) // 16 * 16


def kernel(
    at_hbm, g_hbm, valid_hbm, bi_hbm, bo_hbm, eo_hbm, ei_hbm, prev_in_hbm, prev_out_hbm,
    fin_out, fout_out, pre_out,
    a_all, g_all, gt, bi, bo, bit,
    keeps, c_sends, c_recvs, y_sends, y_recvs, z_sends, z_recvs, o_sends, o_recvs, l_recv, i_send, i_recv,
    at_ref, valid_ref, eo_ref, ei_ref, prev_in_ref, prev_out_ref, fin_ref, fout_ref, pre_ref,
    ar_part, ar, chosen, g_raw, m_keep, mc_send, mc_recv, my_send, my_recv, mz_send, mz_recv, mx,
    qx_send, qx_recv, qz_send, qz, qy, qc,
    n_c, n_y, n_z, n_total,
    send_sem, recv_sem, load_sem,
):
    tm, dp, x = lax.axis_index("tm"), lax.axis_index("dp"), lax.axis_index("factor")
    y, c = tm // 4, tm % 2
    z = dp * 2 + (tm // 2) % 2
    group = tm * 4 + dp
    unit = group * 4 + x
    left, right, opposite = (x + 3) % 4, (x + 1) % 4, (x + 2) % 4

    def peer(dx=0, dy=0, dz=0, dc=0):
        return device((x + dx) % 4, (y + dy) % 4, (z + dz) % 8, (c + dc) % 2)

    out_dsts = [
        {"tm": u // 16, "dp": (u // 4) % 4, "factor": u % 4}
        for u in [64 * x + 32 * c + 8 * y + i for i in range(8)]
    ]
    out_srcs = [device(unit // 64, (unit // 8) % 4, i, (unit // 32) % 2) for i in range(8)]
    turn_dsts = [device(i, x, z, c) for i in range(4)]
    turn_srcs = [device(y, i, z, c) for i in range(4)]
    own_unit = 64 * x + 32 * c + 8 * y + z
    out_dst = {"tm": own_unit // 16, "dp": (own_unit // 4) % 4, "factor": own_unit % 4}
    out_src = device(unit // 64, (unit // 8) % 4, unit % 8, (unit // 32) % 2)
    in_unit = [64 * x + 16 * y + 2 * z + h for h in range(2)]
    in_dst = [{"tm": u // 16, "dp": (u // 4) % 4, "factor": u % 4} for u in in_unit]
    in_src = [device(unit // 64, (unit // 16) % 4, (unit // 2) % 8, h) for h in range(2)]

    def same(d):
        return (d["tm"] == tm) & (d["dp"] == dp) & (d["factor"] == x)

    wanted = (
        (valid_hbm, valid_ref), (at_hbm, at_ref), (g_hbm, g_raw), (bi_hbm, bi), (bo_hbm, bo),
        (eo_hbm, eo_ref), (ei_hbm, ei_ref), (prev_in_hbm, prev_in_ref), (prev_out_hbm, prev_out_ref),
    )
    loads = [pltpu.make_async_copy(*pair, load_sem.at[i]) for i, pair in enumerate(wanted)]
    load_valid, load_at, load_g, load_bi, load_bo = loads[:5]
    load_valid.start()
    load_at.start()

    barrier = pltpu.get_barrier_semaphore()
    peers = [peer(dx=i) for i in (1, 2, 3)] + [peer(dy=i) for i in (1, 2, 3)]
    peers += [peer(dz=i) for i in range(1, 8)] + [peer(dc=1)]
    for d in peers:
        pl.semaphore_signal(barrier, inc=1, device_id=d, device_id_type=MESH)
    for d in turn_srcs + out_srcs + in_src:

        @pl.when(jnp.logical_not(same(d)))
        def _():
            pl.semaphore_signal(barrier, inc=1, device_id=d, device_id_type=MESH)

    expected = len(peers)
    for d in turn_dsts + out_dsts + in_dst:
        expected = expected + jnp.where(same(d), 0, 1)

    for load in loads[2:]:
        load.start()
    load_valid.wait()
    load_at.wait()
    length = jnp.sum(valid_ref[...], keepdims=True)
    a_all[x] = jnp.where(
        lax.broadcasted_iota(jnp.int32, (WA, FR), 1) < length, at_ref[...], jnp.zeros((), BF16)
    )
    n_c[0] = jnp.broadcast_to(length.astype(F32), (8, 128))
    qz_send[...] = jnp.zeros_like(qz_send)
    pl.semaphore_wait(barrier, expected)

    count = [0]
    started = []

    def fresh():
        count[0] += 1
        return count[0] - 1

    def send(src, dst, to, k, alone=True):
        copy = pltpu.make_async_remote_copy(
            src_ref=src, dst_ref=dst, send_sem=send_sem.at[k], recv_sem=recv_sem.at[k],
            device_id=to, device_id_type=MESH,
        )
        copy.start()
        if alone:
            started.append(copy)

    def described(ref, k):
        return pltpu.make_async_remote_copy(
            src_ref=ref, dst_ref=ref, send_sem=send_sem.at[k], recv_sem=recv_sem.at[k],
            device_id=peer(dx=1), device_id_type=MESH,
        )

    def landed(dst, k):
        described(dst, k).wait_recv()

    def send_all(pairs, received, k):
        for src, dst, to in pairs:
            send(src, dst, to, k, alone=False)
        started.append(described(received, k))

    def part(buf, shard, h, cols=None):
        rows = buf.shape[1] // 2
        rows = pl.ds(0, buf.shape[1]) if h is None else pl.ds(h * rows, rows)
        return buf.at[shard, rows] if cols is None else buf.at[shard, rows, cols]

    ka = [fresh() for _ in range(6)]
    kg = [fresh() for _ in range(8)]
    near_cols, last_cols = slice(0, 384), slice(384, 640)

    def both(buf, k, to_right, to_left, cols=None):
        for shard, h, i in ((x, to_right, 1), (x, to_left, 3)):
            at = part(buf, shard, h, cols)
            send(at, at, peer(dx=i), k[i // 2])

    def both_landed(buf, k, from_left, from_right, cols=None):
        landed(part(buf, left, from_left, cols), k[0])
        landed(part(buf, right, from_right, cols), k[1])

    def onward(buf, k, cols=None):
        send(part(buf, left, 0, cols), part(buf, left, 0, cols), peer(dx=1), k[0])
        send(part(buf, right, 1, cols), part(buf, right, 1, cols), peer(dx=3), k[1])

    def far_landed(buf, k, cols=None):
        landed(part(buf, opposite, 0, cols), k[0])
        landed(part(buf, opposite, 1, cols), k[1])

    both(a_all, ka[0:2], 0, 1)
    both(a_all, ka[2:4], 1, 0)

    kc, ky, kz = fresh(), fresh(), fresh()
    n_y_others, n_z_others = n_y.at[pl.ds(1, 3)], n_z.at[pl.ds(1, 7)]
    send(n_c.at[0], n_c.at[1], peer(dc=1), kc)

    def count_y():
        landed(n_c.at[1], kc)
        n_y[0] = n_c[0] + n_c[1]
        pairs = [(n_y.at[0], n_y.at[i + 1], peer(dy=i + 1)) for i in range(3)]
        send_all(pairs, n_y_others, ky)

    def count_z():
        landed(n_y_others, ky)
        n_z[0] = n_y[0] + n_y[1] + n_y[2] + n_y[3]
        pairs = [(n_z.at[0], n_z.at[i + 1], peer(dz=i + 1)) for i in range(7)]
        send_all(pairs, n_z_others, kz)

    def count_done():
        landed(n_z_others, kz)
        total = n_z[0]
        for i in range(7):
            total = total + n_z[i + 1]
        n_total[...] = total

    class Scatter:
        def __init__(self, b):
            self.tiles = WIDTHS[b] // 128
            self.keep, self.c_send, self.c_recv = keeps[b], c_sends[b], c_recvs[b]
            self.y_send, self.y_recv = y_sends[b], y_recvs[b]
            self.z_send, self.z_recv = z_sends[b], z_recvs[b]
            self.o_send, self.o_recv = o_sends[b], o_recvs[b]
            self.kc, self.ky, self.kz, self.ko = fresh(), fresh(), fresh(), fresh()
            self.y_others = self.y_recv.at[pl.ds(0, 3)]

        def core(self, half):
            self.c_send[...] = half(1 - c).astype(BF16)
            send(self.c_send, self.c_recv, peer(dc=1), self.kc)
            self.keep[...] = half(c)

        def along_y(self):
            landed(self.c_recv, self.kc)
            total = self.keep[...] + self.c_recv[...].astype(F32)
            self.keep[...] = total
            self.y_send[...] = total.astype(BF16)
            pairs = []
            for i in range(3):
                rows = pl.ds(pl.multiple_of((y + i + 1) % 4 * 80, 16), 80)
                pairs.append((self.y_send.at[rows], self.y_recv.at[i], peer(dy=i + 1)))
            send_all(pairs, self.y_others, self.ky)

        def sum_y(self):
            total = self.keep[pl.ds(pl.multiple_of(y * 80, 16), 80)]
            landed(self.y_others, self.ky)
            for i in range(3):
                total = total + self.y_recv[i].astype(F32)
            return total

        def pack_z(self):
            total = self.sum_y()
            for i in range(8):
                pieces = [
                    total[10 * i : 10 * i + 10, 128 * j : 128 * j + 128] for j in range(self.tiles)
                ]
                pieces = jnp.concatenate(pieces, axis=0).astype(BF16)
                self.z_send[i, : 10 * self.tiles] = pieces

        def along_z(self):
            self.pack_z()
            pairs = [
                (self.z_send.at[(z + i + 1) % 8], self.z_recv.at[i], peer(dz=i + 1))
                for i in range(7)
            ]
            send_all(pairs, self.z_recv, self.kz)

        def done(self):
            total = self.z_send[z].astype(F32)
            landed(self.z_recv, self.kz)
            for i in range(7):
                total = total + self.z_recv[i].astype(F32)
            return total

        def out_copy(self):
            return pltpu.make_async_remote_copy(
                src_ref=self.o_send, dst_ref=self.o_recv, send_sem=send_sem.at[self.ko],
                recv_sem=recv_sem.at[self.ko], device_id=out_dst, device_id_type=MESH,
            )

        def hand_out(self):
            self.o_send[...] = self.done()
            self_dst = same(out_dst)

            @pl.when(self_dst)
            def _():
                self.o_recv[...] = self.o_send[...]

            @pl.when(jnp.logical_not(self_dst))
            def _():
                self.out_copy().start()

        def handed_out(self):
            @pl.when(jnp.logical_not(same(out_src)))
            def _():
                landed(self.o_recv, self.ko)

            return self.o_recv[...]

    class Spread:
        def __init__(self, src, recv, slot, dsts, srcs):
            self.src, self.recv, self.slot, self.dsts, self.srcs = src, recv, slot, dsts, srcs
            self.k = fresh()
            self.self_dst, self.self_src = (
                functools.reduce(jnp.logical_or, [same(d) for d in to]) for to in (dsts, srcs)
            )

        def start(self):
            for i, d in enumerate(self.dsts):

                @pl.when(same(d))
                def _(i=i):
                    self.recv[self.slot] = self.src(i)[...]

                @pl.when(jnp.logical_not(same(d)))
                def _(i=i, d=d):
                    send(self.src(i), self.recv.at[self.slot], d, self.k, alone=False)

        def wait(self, own, act):
            @pl.when(own)
            def _():
                act(described(self.recv.at[pl.ds(0, len(self.dsts) - 1)], self.k))

            @pl.when(jnp.logical_not(own))
            def _():
                act(described(self.recv, self.k))

        def total(self):
            self.wait(self.self_src, lambda copy: copy.wait_recv())
            total = self.recv[0].astype(F32)
            for i in range(1, len(self.srcs)):
                total = total + self.recv[i].astype(F32)
            return total

        def finish(self):
            self.wait(self.self_dst, lambda copy: copy.wait_send())

    class Straight(Scatter):
        def __init__(self, b):
            super().__init__(b)
            self.spread = Spread(lambda i: self.z_send.at[i], l_recv, z, out_dsts, out_srcs)

        def along_z(self):
            self.pack_z()
            self.spread.start()

        def done(self):
            return self.spread.total()

    class Turned(Scatter):
        def __init__(self, b):
            super().__init__(b)
            self.spread = Spread(
                lambda i: self.y_send.at[pl.ds(80 * i, 80)], self.y_recv, y, turn_dsts, turn_srcs
            )

        def along_y(self):
            landed(self.c_recv, self.kc)
            total = self.keep[...] + self.c_recv[...].astype(F32)
            for i in range(4):
                starts = [(j % 2) * 160 + (j // 2) * 40 + 10 * i for j in range(8)]
                pieces = [total[start : start + 10] for start in starts]
                self.y_send[80 * i : 80 * i + 80] = jnp.concatenate(pieces, axis=0).astype(BF16)
            self.spread.start()

        def sum_y(self):
            return self.spread.total()

    in_rows, own_rows, near_rows, second_rows = (Scatter(i) for i in range(4))
    far_rows, last_rows = Straight(4), Turned(5)
    ki_send = [fresh() for _ in range(2)]
    ki = [fresh() for _ in range(2)]

    def in_copy(h):
        return pltpu.make_async_remote_copy(
            src_ref=i_send.at[h], dst_ref=i_recv.at[c], send_sem=send_sem.at[ki_send[h]],
            recv_sem=recv_sem.at[ki[0] + c], device_id=in_dst[h], device_id_type=MESH,
        )

    def hand_in():
        total = in_rows.done()
        for h in range(2):
            for j in range(5):
                lanes = slice(128 * j, 128 * j + 128)
                i_send[h, :5, lanes] = total[10 * j + 5 * h : 10 * j + 5 * h + 5]
        for h in range(2):
            self_dst = same(in_dst[h])

            @pl.when(self_dst)
            def _(h=h):
                i_recv[c] = i_send[h]

            @pl.when(jnp.logical_not(self_dst))
            def _(h=h):
                in_copy(h).start()

    def own_half(h):
        return dot(gt[pl.ds(pl.multiple_of(h * 320, 16), 320)], g_all[x])

    def near_half(cols):
        def half(h):
            rows = gt[pl.ds(pl.multiple_of(h * 320, 16), 320)]
            sides = [dot(rows, g_all[shard, :, cols]) for shard in (left, right)]
            return jnp.concatenate(sides, axis=1)

        return half

    def far_half(h):
        rows = gt[pl.ds(pl.multiple_of(h * 320, 16), 320)]
        return dot(rows, g_all[opposite, :, near_cols])

    def last_half(h):
        rows = [gt[pl.ds(pl.multiple_of(i * 320 + h * 160, 16), 160)] for i in range(2)]
        return dot(jnp.concatenate(rows, axis=0), g_all[opposite, :, last_cols])

    def in_block(h):
        other = a_all[pl.ds(2 * h, 2)].reshape(2 * WA, FR)
        return dot_nt(a_all[x], other)

    load_g.wait()
    g_all[x] = jnp.where(
        lax.broadcasted_iota(jnp.int32, (FR, WG), 0) < length, g_raw[...], jnp.zeros((), BF16)
    )
    gt[...] = g_all[x].T
    own_rows.core(own_half)
    count_y()
    for buf in z_sends:
        buf[...] = jnp.zeros_like(buf)
    mz_send[...] = jnp.zeros_like(mz_send)
    i_send[...] = jnp.zeros_like(i_send)
    own_rows.along_y()
    count_z()
    both_landed(a_all, ka[0:2], 0, 1)
    onward(a_all, ka[4:6])
    both(g_all, kg[0:2], None, None, near_cols)
    load_bi.wait()
    for i in range(4):
        bit[i] = bi[i * WA : (i + 1) * WA].T

    line = lax.broadcasted_iota(jnp.int32, (256, WG), 0)
    slot, at_z = line % 32, line // 32
    source = (at_z % 2) * 320 + (at_z // 2) * 40 + jnp.where(slot >= 10, 150, 0) + slot
    source = jnp.where(slot < 20, source, -WG)
    ahead = lax.broadcasted_iota(jnp.int32, (256, WG), 1) - source
    for i in range(4):
        chosen[i] = (ahead == 10 * i).astype(F32).astype(BF16)
    own_rows.along_z()
    count_done()
    both_landed(a_all, ka[2:4], 1, 0)

    def rotate_near(t, carry):
        rows = pl.ds(pl.multiple_of(t * 320, 16), 320)
        total = dot(bit[x, rows], a_all[x]) + dot(bit[left, rows], a_all[left])
        ar_part[rows] = total + dot(bit[right, rows], a_all[right])
        return carry

    lax.fori_loop(0, 4, rotate_near, 0)
    far_landed(a_all, ka[4:6])

    def cross(h):
        def rotate_far(t, carry):
            rows = pl.ds(pl.multiple_of(h * 640 + t * 320, 16), 320)
            ar[rows] = (ar_part[rows] + dot(bit[opposite, rows], a_all[opposite])).astype(BF16)
            return carry

        lax.fori_loop(0, 2, rotate_far, 0)
        return dot(ar[pl.ds(pl.multiple_of(h * 640, 16), 640)], g_all[x])

    kmc, kmy, kmz, kmx, kqx = fresh(), fresh(), fresh(), [fresh() for _ in range(3)], fresh()
    mc_send[...] = cross(1 - c).astype(BF16)
    send(mc_send, mc_recv, peer(dc=1), kmc)
    m_keep[...] = cross(c)
    both(g_all, kg[2:4], None, None, last_cols)
    landed(mc_recv, kmc)
    total = m_keep[...] + mc_recv[...].astype(F32)
    m_keep[...] = total
    my_send[...] = total.astype(BF16)
    pairs = []
    for i in range(3):
        rows = pl.ds(pl.multiple_of((y + i + 1) % 4 * 160, 16), 160)
        pairs.append((my_send.at[rows], my_recv.at[i], peer(dy=i + 1)))
    send_all(pairs, my_recv, kmy)
    in_rows.core(in_block)
    own_rows.hand_out()
    for load in loads[4:]:
        load.wait()
    in_rows.along_y()
    total = m_keep[pl.ds(pl.multiple_of(y * 160, 16), 160)]
    landed(my_recv, kmy)
    for i in range(3):
        total = total + my_recv[i].astype(F32)
    for i in range(8):
        pieces = [total[20 * i : 20 * i + 20, 128 * j : 128 * j + 128] for j in range(5)]
        mz_send[i, :100] = jnp.concatenate(pieces, axis=0).astype(BF16)
    pairs = [(mz_send.at[(z + i + 1) % 8], mz_recv.at[i], peer(dz=i + 1)) for i in range(7)]
    send_all(pairs, mz_recv, kmz)
    both_landed(g_all, kg[0:2], None, None, near_cols)
    near_rows.core(near_half(near_cols))
    frames = n_total[:1, :1]
    row = lax.broadcasted_iota(jnp.int32, (20, 1280), 0) + (c * 640 + y * 160 + z * 20)
    here = lax.broadcasted_iota(jnp.int32, (20, 1280), 1) == row
    eigen_rows = jnp.concatenate([ei_ref[i : i + 1] for i in range(10)], axis=1)
    eigen_rows = jnp.sum(jnp.where(here, eigen_rows, 0.0), axis=1, keepdims=True)
    eigen_cols = jnp.concatenate([eo_ref[pl.ds(5 * x + i, 1)] for i in range(5)], axis=1)
    scale = eigen_rows * eigen_cols + damping
    total = mz_send[z].astype(F32)
    landed(mz_recv, kmz)
    for i in range(7):
        total = total + mz_recv[i].astype(F32)

    mx[x] = total.astype(BF16)
    for i in range(3):
        send(mx.at[x], mx.at[x], peer(dx=i + 1), kmx[i])
    onward(g_all, kg[4:6], near_cols)
    in_rows.along_z()
    near_rows.along_y()
    both_landed(g_all, kg[2:4], None, None, last_cols)
    second_rows.core(near_half(last_cols))
    near_rows.along_z()
    for i in range(3):
        landed(mx.at[(x + 3 - i) % 4], kmx[i])
    total = jnp.zeros((20, WG), F32)
    for i in range(4):
        pieces = [mx[i, 20 * j : 20 * j + 20] for j in range(5)]
        total = total + dot(jnp.concatenate(pieces, axis=1), bo[i * WG : (i + 1) * WG])
    scaled = (total / frames / scale).astype(BF16)
    kqz = [fresh() for _ in range(7)]
    kqy, kqc = [fresh() for _ in range(3)], fresh()
    turned = dot_nt(scaled, bo[...]).astype(BF16)
    turned = jnp.concatenate([turned[:, WG * i : WG * i + WG] for i in range(4)], axis=0)
    for i in range(4):
        qx_send[i] = dot_nt(turned, chosen[i]).astype(BF16)
    pairs = [(qx_send.at[(x + i + 1) % 4], qx_recv.at[i], peer(dx=i + 1)) for i in range(3)]
    send_all(pairs, qx_recv, kqx)
    onward(g_all, kg[6:8], last_cols)
    second_rows.along_y()
    hand_in()
    near_rows.hand_out()
    far_landed(g_all, kg[4:6], near_cols)
    far_rows.core(far_half)
    total = qx_send[x].astype(F32)
    landed(qx_recv, kqx)
    for i in range(3):
        total = total + qx_recv[i].astype(F32)
    for i in range(8):
        lanes = slice(32 * i, 32 * i + 32)
        pieces = [total[20 * j : 20 * j + 20, lanes] for j in range(4)]
        qz_send[i, :20] = jnp.concatenate(pieces, axis=1).astype(BF16)
    qz[z] = qz_send[z]
    for i in range(7):
        send(qz_send.at[(z + i + 1) % 8], qz.at[z], peer(dz=i + 1), kqz[i])
    second_rows.along_z()
    far_rows.along_y()
    far_landed(g_all, kg[6:8], last_cols)
    last_rows.core(last_half)
    for i in range(7):
        landed(qz.at[(z + 7 - i) % 8], kqz[i])
    for i in range(8):
        qy[y, 20 * i : 20 * i + 20] = qz[i, :20]
    for i in range(3):
        send(qy.at[y], qy.at[y], peer(dy=i + 1), kqy[i])
    second_rows.hand_out()
    last_rows.along_y()
    far_rows.along_z()
    for i in range(3):
        landed(qy.at[(y + 3 - i) % 4], kqy[i])
    qc[c] = qy[...].reshape(640, 128)
    send(qc.at[c], qc.at[c], peer(dc=1), kqc)
    last_rows.along_z()
    landed(qc.at[1 - c], kqc)
    mine = lax.broadcasted_iota(jnp.int32, (16, 128), 0) + (y * 32 + c * 10)
    mine = lax.broadcasted_iota(jnp.int32, (16, 128), 1) == mine
    picked = dot_nt(mine.astype(F32).astype(BF16), qc[...].reshape(1280, 128)).astype(BF16)
    pre_ref[...] = dot_nt(picked, bi[...])[:10].astype(BF16)
    stores = [
        pltpu.make_async_copy(pair[0], pair[1], load_sem.at[9 + i])
        for i, pair in enumerate(((pre_ref, pre_out), (fin_ref, fin_out), (fout_ref, fout_out)))
    ]
    stores[0].start()

    for h in range(2):

        @pl.when(jnp.logical_not(same(in_src[h])))
        def _(h=h):
            landed(i_recv.at[h], ki[h])

        cols = slice(640 * h, 640 * h + 640)
        fin_ref[:, cols] = factor_decay * prev_in_ref[:, cols] + (1.0 - factor_decay) * (
            i_recv[h, :5] / frames
        )
    stores[1].start()
    source = unit // 64

    def write_out(places, total):
        for j, (step, lane) in enumerate(places):
            at = pl.multiple_of(((source + step) % 4) * WG, 128) + lane
            lanes = pl.ds(pl.multiple_of(at, 128), 128)
            fout_ref[:, lanes] = factor_decay * prev_out_ref[:, lanes] + (1.0 - factor_decay) * (
                total[10 * j : 10 * j + 10] / frames
            )

    def tiles(step, cols=None):
        start, stop = (0, WG) if cols is None else (cols.start, cols.stop)
        return [(step, lane) for lane in range(start, stop, 128)]

    write_out(tiles(0), own_rows.handed_out())
    write_out(tiles(3, near_cols) + tiles(1, near_cols), near_rows.handed_out())
    write_out(tiles(3, last_cols) + tiles(1, last_cols), second_rows.handed_out())
    write_out(tiles(2, near_cols), far_rows.done())
    write_out(tiles(2, last_cols), last_rows.done())
    stores[2].start()

    for copy in started:
        copy.wait_send()
    @pl.when(jnp.logical_not(same(out_dst)))
    def _():
        for rows in (own_rows, near_rows, second_rows):
            rows.out_copy().wait_send()

    far_rows.spread.finish()
    last_rows.spread.finish()
    for h in range(2):

        @pl.when(jnp.logical_not(same(in_dst[h])))
        def _(h=h):
            in_copy(h).wait_send()

    for store in stores:
        store.wait()
    assert count[0] <= MESSAGES, count[0]


def handed_on(*refs):
    for i in range(3):
        refs[3 + i][...] = refs[i][...]


def shards(
    activations, gradients, valid_frames, basis_in, basis_out, eigen_in, eigen_out,
    previous_in, previous_out,
):
    vmem = pl.BlockSpec(memory_space=pltpu.VMEM)
    hbm = pl.BlockSpec(memory_space=pl.ANY)
    V = pltpu.VMEM
    results = pl.pallas_call(
        kernel,
        out_shape=(
            jax.ShapeDtypeStruct(previous_in.shape, F32),
            jax.ShapeDtypeStruct(previous_out.shape, F32),
            jax.ShapeDtypeStruct((10, 1280), BF16),
        ),
        in_specs=[hbm] * 9,
        out_specs=(hbm, hbm, hbm),
        scratch_shapes=[
            V((4, WA, FR), BF16), V((4, FR, WG), BF16), V((WG, FR), BF16),
            V((1280, 1280), BF16), V((2560, WG), BF16), V((4, 1280, WA), BF16),
            [V((320, w), F32) for w in WIDTHS], [V((320, w), BF16) for w in WIDTHS],
            [V((320, w), BF16) for w in WIDTHS], [V((320, w), BF16) for w in WIDTHS],
            [V((4, 80, w), BF16) for w in WIDTHS], [V((8, lines_of(w), 128), BF16) for w in WIDTHS],
            [V((7, lines_of(w), 128), BF16) for w in WIDTHS],
            [V((lines_of(w), 128), F32) for w in WIDTHS], [V((lines_of(w), 128), F32) for w in WIDTHS],
            V((8, lines_of(WIDTHS[4]), 128), BF16), V((2, 8, 640), F32), V((2, 8, 640), F32),
            V((WA, FR), BF16), V((8, 128), jnp.int32), V((20, 128), F32), V((10, 128), F32),
            V((5, 1280), F32), V((10, 2560), F32),
            V((5, 1280), F32), V((10, 2560), F32), V((10, 1280), BF16),
            V((1280, FR), F32), V((1280, FR), BF16), V((4, 256, WG), BF16),
            V((FR, WG), BF16),
            V((640, 640), F32), V((640, 640), BF16), V((640, 640), BF16),
            V((640, 640), BF16), V((3, 160, 640), BF16),
            V((8, 112, 128), BF16), V((7, 112, 128), BF16),
            V((4, 112, 128), BF16),
            V((4, 80, 256), BF16), V((3, 80, 256), BF16), V((8, 32, 128), BF16),
            V((8, 32, 128), BF16), V((4, 160, 128), BF16), V((2, 640, 128), BF16),
            V((2, 8, 128), F32), V((4, 8, 128), F32), V((8, 8, 128), F32),
            V((8, 128), F32),
            pltpu.SemaphoreType.DMA((MESSAGES,)), pltpu.SemaphoreType.DMA((MESSAGES,)),
            pltpu.SemaphoreType.DMA((12,)),
        ],
        compiler_params=pltpu.CompilerParams(
            collective_id=0, has_side_effects=True, vmem_limit_bytes=60 * 1024 * 1024
        ),
    )(
        activations.T, gradients, valid_frames.reshape(8, 128), basis_in, basis_out,
        eigen_out.reshape(20, 128), eigen_in.reshape(10, 128), previous_in, previous_out,
    )
    return pl.pallas_call(
        handed_on,
        out_shape=[jax.ShapeDtypeStruct(r.shape, r.dtype) for r in results],
        in_specs=[vmem] * 3,
        out_specs=[vmem] * 3,
    )(*results)


def solution(mesh):
    rows = P(("tm", "dp", "factor"), None)
    in_specs = (
        P(("tm", "dp"), "factor"),
        P(("tm", "dp"), "factor"),
        P(("tm", "dp")),
        P(),
        P(None, "factor"),
        P(),
        P(),
        rows,
        rows,
    )
    return jax.shard_map(
        shards, mesh=mesh, in_specs=in_specs, out_specs=(rows, rows, rows), check_vma=False
    )
```

```python
import functools

import jax
import jax.numpy as jnp
from jax import lax
from jax.experimental import pallas as pl
from jax.experimental.pallas import tpu as pltpu
from jax.sharding import PartitionSpec as P

factor_decay = 0.5
damping = 0.001
MESH = pl.DeviceIdType.MESH
F32 = jnp.float32
BF16 = jnp.bfloat16

FR = 1024
WA = 320
WG = 640
MESSAGES = 65


def device(x, y, z, c):
    return {"tm": y * 4 + (z % 2) * 2 + c, "dp": z // 2, "factor": x}


def dot(left, right):
    return jnp.dot(left, right, preferred_element_type=F32)


def dot_nt(left, right):
    return lax.dot_general(left, right, (((1,), (1,)), ((), ())), preferred_element_type=F32)


WIDTHS = (640, 640, 1024, 256, 512, 128)


def lines_of(width):
    return (10 * (width // 128) + 15) // 16 * 16


def kernel(
    at_hbm, g_hbm, valid_hbm, bi_hbm, bo_hbm, eo_hbm, ei_hbm, prev_in_hbm, prev_out_hbm,
    fin_out, fout_out, pre_out,
    a_all, g_all, gt, bi, bo, bit,
    keeps, c_sends, c_recvs, y_sends, y_recvs, z_sends, z_recvs, o_sends, o_recvs, l_recv, i_send, i_recv,
    at_ref, valid_ref, eo_ref, ei_ref, prev_in_ref, prev_out_ref, fin_ref, fout_ref, pre_ref,
    ar_part, ar, chosen, g_raw, m_keep, mc_send, mc_recv, my_send, my_recv, mz_send, mz_recv, mx,
    qx_send, qx_recv, qz_send, qz, qy, qc,
    n_c, n_y, n_z, n_total,
    send_sem, recv_sem, load_sem,
):
    tm, dp, x = lax.axis_index("tm"), lax.axis_index("dp"), lax.axis_index("factor")
    y, c = tm // 4, tm % 2
    z = dp * 2 + (tm // 2) % 2
    group = tm * 4 + dp
    unit = group * 4 + x
    left, right, opposite = (x + 3) % 4, (x + 1) % 4, (x + 2) % 4

    def peer(dx=0, dy=0, dz=0, dc=0):
        return device((x + dx) % 4, (y + dy) % 4, (z + dz) % 8, (c + dc) % 2)

    out_dsts = [
        {"tm": u // 16, "dp": (u // 4) % 4, "factor": u % 4}
        for u in [64 * x + 32 * c + 8 * y + i for i in range(8)]
    ]
    out_srcs = [device(unit // 64, (unit // 8) % 4, i, (unit // 32) % 2) for i in range(8)]
    turn_dsts = [device(i, x, z, c) for i in range(4)]
    turn_srcs = [device(y, i, z, c) for i in range(4)]
    own_unit = 64 * x + 32 * c + 8 * y + z
    out_dst = {"tm": own_unit // 16, "dp": (own_unit // 4) % 4, "factor": own_unit % 4}
    out_src = device(unit // 64, (unit // 8) % 4, unit % 8, (unit // 32) % 2)
    in_unit = [64 * x + 16 * y + 2 * z + h for h in range(2)]
    in_dst = [{"tm": u // 16, "dp": (u // 4) % 4, "factor": u % 4} for u in in_unit]
    in_src = [device(unit // 64, (unit // 16) % 4, (unit // 2) % 8, h) for h in range(2)]

    def same(d):
        return (d["tm"] == tm) & (d["dp"] == dp) & (d["factor"] == x)

    wanted = (
        (valid_hbm, valid_ref), (at_hbm, at_ref), (g_hbm, g_raw), (bi_hbm, bi), (bo_hbm, bo),
        (eo_hbm, eo_ref), (ei_hbm, ei_ref), (prev_in_hbm, prev_in_ref), (prev_out_hbm, prev_out_ref),
    )
    loads = [pltpu.make_async_copy(*pair, load_sem.at[i]) for i, pair in enumerate(wanted)]
    load_valid, load_at, load_g, load_bi, load_bo = loads[:5]
    load_valid.start()
    load_at.start()

    barrier = pltpu.get_barrier_semaphore()
    peers = [peer(dx=i) for i in (1, 2, 3)] + [peer(dy=i) for i in (1, 2, 3)]
    peers += [peer(dz=i) for i in range(1, 8)] + [peer(dc=1)]
    for d in peers:
        pl.semaphore_signal(barrier, inc=1, device_id=d, device_id_type=MESH)
    for d in turn_srcs + out_srcs + in_src:

        @pl.when(jnp.logical_not(same(d)))
        def _():
            pl.semaphore_signal(barrier, inc=1, device_id=d, device_id_type=MESH)

    expected = len(peers)
    for d in turn_dsts + out_dsts + in_dst:
        expected = expected + jnp.where(same(d), 0, 1)

    for load in loads[2:]:
        load.start()
    load_valid.wait()
    load_at.wait()
    length = jnp.sum(valid_ref[...], keepdims=True)
    a_all[x] = jnp.where(
        lax.broadcasted_iota(jnp.int32, (WA, FR), 1) < length, at_ref[...], jnp.zeros((), BF16)
    )
    n_c[0] = jnp.broadcast_to(length.astype(F32), (8, 128))
    qz_send[...] = jnp.zeros_like(qz_send)
    pl.semaphore_wait(barrier, expected)

    count = [0]
    started = []

    def fresh():
        count[0] += 1
        return count[0] - 1

    def send(src, dst, to, k, alone=True):
        copy = pltpu.make_async_remote_copy(
            src_ref=src, dst_ref=dst, send_sem=send_sem.at[k], recv_sem=recv_sem.at[k],
            device_id=to, device_id_type=MESH,
        )
        copy.start()
        if alone:
            started.append(copy)

    def described(ref, k):
        return pltpu.make_async_remote_copy(
            src_ref=ref, dst_ref=ref, send_sem=send_sem.at[k], recv_sem=recv_sem.at[k],
            device_id=peer(dx=1), device_id_type=MESH,
        )

    def landed(dst, k):
        described(dst, k).wait_recv()

    def send_all(pairs, received, k):
        for src, dst, to in pairs:
            send(src, dst, to, k, alone=False)
        started.append(described(received, k))

    def part(buf, shard, h, cols=None):
        rows = buf.shape[1] // 2
        rows = pl.ds(0, buf.shape[1]) if h is None else pl.ds(h * rows, rows)
        return buf.at[shard, rows] if cols is None else buf.at[shard, rows, cols]

    ka = [fresh() for _ in range(6)]
    kg = [fresh() for _ in range(8)]
    near_cols, last_cols = slice(0, 512), slice(512, 640)

    def both(buf, k, to_right, to_left, cols=None):
        for shard, h, i in ((x, to_right, 1), (x, to_left, 3)):
            at = part(buf, shard, h, cols)
            send(at, at, peer(dx=i), k[i // 2])

    def both_landed(buf, k, from_left, from_right, cols=None):
        landed(part(buf, left, from_left, cols), k[0])
        landed(part(buf, right, from_right, cols), k[1])

    def onward(buf, k, cols=None):
        send(part(buf, left, 0, cols), part(buf, left, 0, cols), peer(dx=1), k[0])
        send(part(buf, right, 1, cols), part(buf, right, 1, cols), peer(dx=3), k[1])

    def far_landed(buf, k, cols=None):
        landed(part(buf, opposite, 0, cols), k[0])
        landed(part(buf, opposite, 1, cols), k[1])

    both(a_all, ka[0:2], 0, 1)
    both(a_all, ka[2:4], 1, 0)

    kc, ky, kz = fresh(), fresh(), fresh()
    n_y_others, n_z_others = n_y.at[pl.ds(1, 3)], n_z.at[pl.ds(1, 7)]
    send(n_c.at[0], n_c.at[1], peer(dc=1), kc)

    def count_y():
        landed(n_c.at[1], kc)
        n_y[0] = n_c[0] + n_c[1]
        pairs = [(n_y.at[0], n_y.at[i + 1], peer(dy=i + 1)) for i in range(3)]
        send_all(pairs, n_y_others, ky)

    def count_z():
        landed(n_y_others, ky)
        n_z[0] = n_y[0] + n_y[1] + n_y[2] + n_y[3]
        pairs = [(n_z.at[0], n_z.at[i + 1], peer(dz=i + 1)) for i in range(7)]
        send_all(pairs, n_z_others, kz)

    def count_done():
        landed(n_z_others, kz)
        total = n_z[0]
        for i in range(7):
            total = total + n_z[i + 1]
        n_total[...] = total

    class Scatter:
        def __init__(self, b):
            self.tiles = WIDTHS[b] // 128
            self.keep, self.c_send, self.c_recv = keeps[b], c_sends[b], c_recvs[b]
            self.y_send, self.y_recv = y_sends[b], y_recvs[b]
            self.z_send, self.z_recv = z_sends[b], z_recvs[b]
            self.o_send, self.o_recv = o_sends[b], o_recvs[b]
            self.kc, self.ky, self.kz, self.ko = fresh(), fresh(), fresh(), fresh()
            self.y_others = self.y_recv.at[pl.ds(0, 3)]

        def core(self, half):
            self.c_send[...] = half(1 - c).astype(BF16)
            send(self.c_send, self.c_recv, peer(dc=1), self.kc)
            self.keep[...] = half(c)

        def along_y(self):
            landed(self.c_recv, self.kc)
            total = self.keep[...] + self.c_recv[...].astype(F32)
            self.keep[...] = total
            self.y_send[...] = total.astype(BF16)
            pairs = []
            for i in range(3):
                rows = pl.ds(pl.multiple_of((y + i + 1) % 4 * 80, 16), 80)
                pairs.append((self.y_send.at[rows], self.y_recv.at[i], peer(dy=i + 1)))
            send_all(pairs, self.y_others, self.ky)

        def sum_y(self):
            total = self.keep[pl.ds(pl.multiple_of(y * 80, 16), 80)]
            landed(self.y_others, self.ky)
            for i in range(3):
                total = total + self.y_recv[i].astype(F32)
            return total

        def pack_z(self):
            total = self.sum_y()
            for i in range(8):
                pieces = [
                    total[10 * i : 10 * i + 10, 128 * j : 128 * j + 128] for j in range(self.tiles)
                ]
                pieces = jnp.concatenate(pieces, axis=0).astype(BF16)
                self.z_send[i, : 10 * self.tiles] = pieces

        def along_z(self):
            self.pack_z()
            pairs = [
                (self.z_send.at[(z + i + 1) % 8], self.z_recv.at[i], peer(dz=i + 1))
                for i in range(7)
            ]
            send_all(pairs, self.z_recv, self.kz)

        def done(self):
            total = self.z_send[z].astype(F32)
            landed(self.z_recv, self.kz)
            for i in range(7):
                total = total + self.z_recv[i].astype(F32)
            return total

        def out_copy(self):
            return pltpu.make_async_remote_copy(
                src_ref=self.o_send, dst_ref=self.o_recv, send_sem=send_sem.at[self.ko],
                recv_sem=recv_sem.at[self.ko], device_id=out_dst, device_id_type=MESH,
            )

        def hand_out(self):
            self.o_send[...] = self.done()
            self_dst = same(out_dst)

            @pl.when(self_dst)
            def _():
                self.o_recv[...] = self.o_send[...]

            @pl.when(jnp.logical_not(self_dst))
            def _():
                self.out_copy().start()

        def handed_out(self):
            @pl.when(jnp.logical_not(same(out_src)))
            def _():
                landed(self.o_recv, self.ko)

            return self.o_recv[...]

    class Spread:
        def __init__(self, src, recv, slot, dsts, srcs):
            self.src, self.recv, self.slot, self.dsts, self.srcs = src, recv, slot, dsts, srcs
            self.k = fresh()
            self.self_dst, self.self_src = (
                functools.reduce(jnp.logical_or, [same(d) for d in to]) for to in (dsts, srcs)
            )

        def start(self):
            for i, d in enumerate(self.dsts):

                @pl.when(same(d))
                def _(i=i):
                    self.recv[self.slot] = self.src(i)[...]

                @pl.when(jnp.logical_not(same(d)))
                def _(i=i, d=d):
                    send(self.src(i), self.recv.at[self.slot], d, self.k, alone=False)

        def wait(self, own, act):
            @pl.when(own)
            def _():
                act(described(self.recv.at[pl.ds(0, len(self.dsts) - 1)], self.k))

            @pl.when(jnp.logical_not(own))
            def _():
                act(described(self.recv, self.k))

        def total(self):
            self.wait(self.self_src, lambda copy: copy.wait_recv())
            total = self.recv[0].astype(F32)
            for i in range(1, len(self.srcs)):
                total = total + self.recv[i].astype(F32)
            return total

        def finish(self):
            self.wait(self.self_dst, lambda copy: copy.wait_send())

    class Straight(Scatter):
        def __init__(self, b):
            super().__init__(b)
            self.spread = Spread(lambda i: self.z_send.at[i], l_recv, z, out_dsts, out_srcs)

        def along_z(self):
            self.pack_z()
            self.spread.start()

        def done(self):
            return self.spread.total()

    class Turned(Scatter):
        def __init__(self, b):
            super().__init__(b)
            self.spread = Spread(
                lambda i: self.y_send.at[pl.ds(80 * i, 80)], self.y_recv, y, turn_dsts, turn_srcs
            )

        def along_y(self):
            landed(self.c_recv, self.kc)
            total = self.keep[...] + self.c_recv[...].astype(F32)
            for i in range(4):
                starts = [(j % 2) * 160 + (j // 2) * 40 + 10 * i for j in range(8)]
                pieces = [total[start : start + 10] for start in starts]
                self.y_send[80 * i : 80 * i + 80] = jnp.concatenate(pieces, axis=0).astype(BF16)
            self.spread.start()

        def sum_y(self):
            return self.spread.total()

    in_rows, own_rows, near_rows, second_rows = (Scatter(i) for i in range(4))
    far_rows, last_rows = Straight(4), Turned(5)
    ki_send = [fresh() for _ in range(2)]
    ki = [fresh() for _ in range(2)]

    def in_copy(h):
        return pltpu.make_async_remote_copy(
            src_ref=i_send.at[h], dst_ref=i_recv.at[c], send_sem=send_sem.at[ki_send[h]],
            recv_sem=recv_sem.at[ki[0] + c], device_id=in_dst[h], device_id_type=MESH,
        )

    def hand_in():
        total = in_rows.done()
        for h in range(2):
            for j in range(5):
                lanes = slice(128 * j, 128 * j + 128)
                i_send[h, :5, lanes] = total[10 * j + 5 * h : 10 * j + 5 * h + 5]
        for h in range(2):
            self_dst = same(in_dst[h])

            @pl.when(self_dst)
            def _(h=h):
                i_recv[c] = i_send[h]

            @pl.when(jnp.logical_not(self_dst))
            def _(h=h):
                in_copy(h).start()

    def own_half(h):
        return dot(gt[pl.ds(pl.multiple_of(h * 320, 16), 320)], g_all[x])

    def near_half(cols):
        def half(h):
            rows = gt[pl.ds(pl.multiple_of(h * 320, 16), 320)]
            sides = [dot(rows, g_all[shard, :, cols]) for shard in (left, right)]
            return jnp.concatenate(sides, axis=1)

        return half

    def far_half(h):
        rows = gt[pl.ds(pl.multiple_of(h * 320, 16), 320)]
        return dot(rows, g_all[opposite, :, near_cols])

    def last_half(h):
        rows = [gt[pl.ds(pl.multiple_of(i * 320 + h * 160, 16), 160)] for i in range(2)]
        return dot(jnp.concatenate(rows, axis=0), g_all[opposite, :, last_cols])

    def in_block(h):
        other = a_all[pl.ds(2 * h, 2)].reshape(2 * WA, FR)
        return dot_nt(a_all[x], other)

    load_g.wait()
    g_all[x] = jnp.where(
        lax.broadcasted_iota(jnp.int32, (FR, WG), 0) < length, g_raw[...], jnp.zeros((), BF16)
    )
    gt[...] = g_all[x].T
    own_rows.core(own_half)
    count_y()
    for buf in z_sends:
        buf[...] = jnp.zeros_like(buf)
    mz_send[...] = jnp.zeros_like(mz_send)
    i_send[...] = jnp.zeros_like(i_send)
    own_rows.along_y()
    count_z()
    both_landed(a_all, ka[0:2], 0, 1)
    onward(a_all, ka[4:6])
    both(g_all, kg[0:2], None, None, near_cols)
    load_bi.wait()
    for i in range(4):
        bit[i] = bi[i * WA : (i + 1) * WA].T

    line = lax.broadcasted_iota(jnp.int32, (256, WG), 0)
    slot, at_z = line % 32, line // 32
    source = (at_z % 2) * 320 + (at_z // 2) * 40 + jnp.where(slot >= 10, 150, 0) + slot
    source = jnp.where(slot < 20, source, -WG)
    ahead = lax.broadcasted_iota(jnp.int32, (256, WG), 1) - source
    for i in range(4):
        chosen[i] = (ahead == 10 * i).astype(F32).astype(BF16)
    own_rows.along_z()
    count_done()
    both_landed(a_all, ka[2:4], 1, 0)

    def rotate_near(t, carry):
        rows = pl.ds(pl.multiple_of(t * 320, 16), 320)
        total = dot(bit[x, rows], a_all[x]) + dot(bit[left, rows], a_all[left])
        ar_part[rows] = total + dot(bit[right, rows], a_all[right])
        return carry

    lax.fori_loop(0, 4, rotate_near, 0)
    far_landed(a_all, ka[4:6])

    def cross(h):
        def rotate_far(t, carry):
            rows = pl.ds(pl.multiple_of(h * 640 + t * 320, 16), 320)
            ar[rows] = (ar_part[rows] + dot(bit[opposite, rows], a_all[opposite])).astype(BF16)
            return carry

        lax.fori_loop(0, 2, rotate_far, 0)
        return dot(ar[pl.ds(pl.multiple_of(h * 640, 16), 640)], g_all[x])

    kmc, kmy, kmz, kmx, kqx = fresh(), fresh(), fresh(), [fresh() for _ in range(3)], fresh()
    mc_send[...] = cross(1 - c).astype(BF16)
    send(mc_send, mc_recv, peer(dc=1), kmc)
    m_keep[...] = cross(c)
    both(g_all, kg[2:4], None, None, last_cols)
    landed(mc_recv, kmc)
    total = m_keep[...] + mc_recv[...].astype(F32)
    m_keep[...] = total
    my_send[...] = total.astype(BF16)
    pairs = []
    for i in range(3):
        rows = pl.ds(pl.multiple_of((y + i + 1) % 4 * 160, 16), 160)
        pairs.append((my_send.at[rows], my_recv.at[i], peer(dy=i + 1)))
    send_all(pairs, my_recv, kmy)
    in_rows.core(in_block)
    own_rows.hand_out()
    for load in loads[4:]:
        load.wait()
    in_rows.along_y()
    total = m_keep[pl.ds(pl.multiple_of(y * 160, 16), 160)]
    landed(my_recv, kmy)
    for i in range(3):
        total = total + my_recv[i].astype(F32)
    for i in range(8):
        pieces = [total[20 * i : 20 * i + 20, 128 * j : 128 * j + 128] for j in range(5)]
        mz_send[i, :100] = jnp.concatenate(pieces, axis=0).astype(BF16)
    pairs = [(mz_send.at[(z + i + 1) % 8], mz_recv.at[i], peer(dz=i + 1)) for i in range(7)]
    send_all(pairs, mz_recv, kmz)
    both_landed(g_all, kg[0:2], None, None, near_cols)
    near_rows.core(near_half(near_cols))
    frames = n_total[:1, :1]
    row = lax.broadcasted_iota(jnp.int32, (20, 1280), 0) + (c * 640 + y * 160 + z * 20)
    here = lax.broadcasted_iota(jnp.int32, (20, 1280), 1) == row
    eigen_rows = jnp.concatenate([ei_ref[i : i + 1] for i in range(10)], axis=1)
    eigen_rows = jnp.sum(jnp.where(here, eigen_rows, 0.0), axis=1, keepdims=True)
    eigen_cols = jnp.concatenate([eo_ref[pl.ds(5 * x + i, 1)] for i in range(5)], axis=1)
    scale = eigen_rows * eigen_cols + damping
    total = mz_send[z].astype(F32)
    landed(mz_recv, kmz)
    for i in range(7):
        total = total + mz_recv[i].astype(F32)

    mx[x] = total.astype(BF16)
    for i in range(3):
        send(mx.at[x], mx.at[x], peer(dx=i + 1), kmx[i])
    onward(g_all, kg[4:6], near_cols)
    in_rows.along_z()
    near_rows.along_y()
    both_landed(g_all, kg[2:4], None, None, last_cols)
    second_rows.core(near_half(last_cols))
    near_rows.along_z()
    for i in range(3):
        landed(mx.at[(x + 3 - i) % 4], kmx[i])
    total = jnp.zeros((20, WG), F32)
    for i in range(4):
        pieces = [mx[i, 20 * j : 20 * j + 20] for j in range(5)]
        total = total + dot(jnp.concatenate(pieces, axis=1), bo[i * WG : (i + 1) * WG])
    scaled = (total / frames / scale).astype(BF16)
    kqz = [fresh() for _ in range(7)]
    kqy, kqc = [fresh() for _ in range(3)], fresh()
    turned = dot_nt(scaled, bo[...]).astype(BF16)
    turned = jnp.concatenate([turned[:, WG * i : WG * i + WG] for i in range(4)], axis=0)
    for i in range(4):
        qx_send[i] = dot_nt(turned, chosen[i]).astype(BF16)
    pairs = [(qx_send.at[(x + i + 1) % 4], qx_recv.at[i], peer(dx=i + 1)) for i in range(3)]
    send_all(pairs, qx_recv, kqx)
    onward(g_all, kg[6:8], last_cols)
    second_rows.along_y()
    hand_in()
    near_rows.hand_out()
    far_landed(g_all, kg[4:6], near_cols)
    far_rows.core(far_half)
    total = qx_send[x].astype(F32)
    landed(qx_recv, kqx)
    for i in range(3):
        total = total + qx_recv[i].astype(F32)
    for i in range(8):
        lanes = slice(32 * i, 32 * i + 32)
        pieces = [total[20 * j : 20 * j + 20, lanes] for j in range(4)]
        qz_send[i, :20] = jnp.concatenate(pieces, axis=1).astype(BF16)
    qz[z] = qz_send[z]
    for i in range(7):
        send(qz_send.at[(z + i + 1) % 8], qz.at[z], peer(dz=i + 1), kqz[i])
    second_rows.along_z()
    far_rows.along_y()
    far_landed(g_all, kg[6:8], last_cols)
    last_rows.core(last_half)
    for i in range(7):
        landed(qz.at[(z + 7 - i) % 8], kqz[i])
    for i in range(8):
        qy[y, 20 * i : 20 * i + 20] = qz[i, :20]
    for i in range(3):
        send(qy.at[y], qy.at[y], peer(dy=i + 1), kqy[i])
    second_rows.hand_out()
    last_rows.along_y()
    far_rows.along_z()
    for i in range(3):
        landed(qy.at[(y + 3 - i) % 4], kqy[i])
    qc[c] = qy[...].reshape(640, 128)
    send(qc.at[c], qc.at[c], peer(dc=1), kqc)
    last_rows.along_z()
    landed(qc.at[1 - c], kqc)
    mine = lax.broadcasted_iota(jnp.int32, (16, 128), 0) + (y * 32 + c * 10)
    mine = lax.broadcasted_iota(jnp.int32, (16, 128), 1) == mine
    picked = dot_nt(mine.astype(F32).astype(BF16), qc[...].reshape(1280, 128)).astype(BF16)
    pre_ref[...] = dot_nt(picked, bi[...])[:10].astype(BF16)
    stores = [
        pltpu.make_async_copy(pair[0], pair[1], load_sem.at[9 + i])
        for i, pair in enumerate(((pre_ref, pre_out), (fin_ref, fin_out), (fout_ref, fout_out)))
    ]
    stores[0].start()

    for h in range(2):

        @pl.when(jnp.logical_not(same(in_src[h])))
        def _(h=h):
            landed(i_recv.at[h], ki[h])

        cols = slice(640 * h, 640 * h + 640)
        fin_ref[:, cols] = factor_decay * prev_in_ref[:, cols] + (1.0 - factor_decay) * (
            i_recv[h, :5] / frames
        )
    stores[1].start()
    source = unit // 64

    def write_out(places, total):
        for j, (step, lane) in enumerate(places):
            at = pl.multiple_of(((source + step) % 4) * WG, 128) + lane
            lanes = pl.ds(pl.multiple_of(at, 128), 128)
            fout_ref[:, lanes] = factor_decay * prev_out_ref[:, lanes] + (1.0 - factor_decay) * (
                total[10 * j : 10 * j + 10] / frames
            )

    def tiles(step, cols=None):
        start, stop = (0, WG) if cols is None else (cols.start, cols.stop)
        return [(step, lane) for lane in range(start, stop, 128)]

    write_out(tiles(0), own_rows.handed_out())
    write_out(tiles(3, near_cols) + tiles(1, near_cols), near_rows.handed_out())
    write_out(tiles(3, last_cols) + tiles(1, last_cols), second_rows.handed_out())
    write_out(tiles(2, near_cols), far_rows.done())
    write_out(tiles(2, last_cols), last_rows.done())
    stores[2].start()

    for copy in started:
        copy.wait_send()
    @pl.when(jnp.logical_not(same(out_dst)))
    def _():
        for rows in (own_rows, near_rows, second_rows):
            rows.out_copy().wait_send()

    far_rows.spread.finish()
    last_rows.spread.finish()
    for h in range(2):

        @pl.when(jnp.logical_not(same(in_dst[h])))
        def _(h=h):
            in_copy(h).wait_send()

    for store in stores:
        store.wait()
    assert count[0] <= MESSAGES, count[0]


def handed_on(*refs):
    for i in range(3):
        refs[3 + i][...] = refs[i][...]


def shards(
    activations, gradients, valid_frames, basis_in, basis_out, eigen_in, eigen_out,
    previous_in, previous_out,
):
    vmem = pl.BlockSpec(memory_space=pltpu.VMEM)
    hbm = pl.BlockSpec(memory_space=pl.ANY)
    V = pltpu.VMEM
    results = pl.pallas_call(
        kernel,
        out_shape=(
            jax.ShapeDtypeStruct(previous_in.shape, F32),
            jax.ShapeDtypeStruct(previous_out.shape, F32),
            jax.ShapeDtypeStruct((10, 1280), BF16),
        ),
        in_specs=[hbm] * 9,
        out_specs=(hbm, hbm, hbm),
        scratch_shapes=[
            V((4, WA, FR), BF16), V((4, FR, WG), BF16), V((WG, FR), BF16),
            V((1280, 1280), BF16), V((2560, WG), BF16), V((4, 1280, WA), BF16),
            [V((320, w), F32) for w in WIDTHS], [V((320, w), BF16) for w in WIDTHS],
            [V((320, w), BF16) for w in WIDTHS], [V((320, w), BF16) for w in WIDTHS],
            [V((4, 80, w), BF16) for w in WIDTHS], [V((8, lines_of(w), 128), BF16) for w in WIDTHS],
            [V((7, lines_of(w), 128), BF16) for w in WIDTHS],
            [V((lines_of(w), 128), F32) for w in WIDTHS], [V((lines_of(w), 128), F32) for w in WIDTHS],
            V((8, lines_of(WIDTHS[4]), 128), BF16), V((2, 8, 640), F32), V((2, 8, 640), F32),
            V((WA, FR), BF16), V((8, 128), jnp.int32), V((20, 128), F32), V((10, 128), F32),
            V((5, 1280), F32), V((10, 2560), F32),
            V((5, 1280), F32), V((10, 2560), F32), V((10, 1280), BF16),
            V((1280, FR), F32), V((1280, FR), BF16), V((4, 256, WG), BF16),
            V((FR, WG), BF16),
            V((640, 640), F32), V((640, 640), BF16), V((640, 640), BF16),
            V((640, 640), BF16), V((3, 160, 640), BF16),
            V((8, 112, 128), BF16), V((7, 112, 128), BF16),
            V((4, 112, 128), BF16),
            V((4, 80, 256), BF16), V((3, 80, 256), BF16), V((8, 32, 128), BF16),
            V((8, 32, 128), BF16), V((4, 160, 128), BF16), V((2, 640, 128), BF16),
            V((2, 8, 128), F32), V((4, 8, 128), F32), V((8, 8, 128), F32),
            V((8, 128), F32),
            pltpu.SemaphoreType.DMA((MESSAGES,)), pltpu.SemaphoreType.DMA((MESSAGES,)),
            pltpu.SemaphoreType.DMA((12,)),
        ],
        compiler_params=pltpu.CompilerParams(
            collective_id=0, has_side_effects=True, vmem_limit_bytes=60 * 1024 * 1024
        ),
    )(
        activations.T, gradients, valid_frames.reshape(8, 128), basis_in, basis_out,
        eigen_out.reshape(20, 128), eigen_in.reshape(10, 128), previous_in, previous_out,
    )
    return pl.pallas_call(
        handed_on,
        out_shape=[jax.ShapeDtypeStruct(r.shape, r.dtype) for r in results],
        in_specs=[vmem] * 3,
        out_specs=[vmem] * 3,
    )(*results)


def solution(mesh):
    rows = P(("tm", "dp", "factor"), None)
    in_specs = (
        P(("tm", "dp"), "factor"),
        P(("tm", "dp"), "factor"),
        P(("tm", "dp")),
        P(),
        P(None, "factor"),
        P(),
        P(),
        rows,
        rows,
    )
    return jax.shard_map(
        shards, mesh=mesh, in_specs=in_specs, out_specs=(rows, rows, rows), check_vma=False
    )
```

```python
import functools

import jax
import jax.numpy as jnp
from jax import lax
from jax.experimental import pallas as pl
from jax.experimental.pallas import tpu as pltpu
from jax.sharding import PartitionSpec as P

factor_decay = 0.5
damping = 0.001
MESH = pl.DeviceIdType.MESH
F32 = jnp.float32
BF16 = jnp.bfloat16

FR = 1024
WA = 320
WG = 640
MESSAGES = 65


def device(x, y, z, c):
    return {"tm": y * 4 + (z % 2) * 2 + c, "dp": z // 2, "factor": x}


def dot(left, right):
    return jnp.dot(left, right, preferred_element_type=F32)


def dot_nt(left, right):
    return lax.dot_general(left, right, (((1,), (1,)), ((), ())), preferred_element_type=F32)


WIDTHS = (640, 640, 1024, 256, 512, 128)


def lines_of(width):
    return (10 * (width // 128) + 15) // 16 * 16


def kernel(
    at_hbm, g_hbm, valid_hbm, bi_hbm, bo_hbm, eo_hbm, ei_hbm, prev_in_hbm, prev_out_hbm,
    fin_out, fout_out, pre_out,
    a_all, g_all, gt, bi, bo, bit,
    keeps, c_sends, c_recvs, y_sends, y_recvs, z_sends, z_recvs, o_sends, o_recvs, l_recv, i_send, i_recv,
    at_ref, valid_ref, eo_ref, ei_ref, prev_in_ref, prev_out_ref, fin_ref, fout_ref, pre_ref,
    ar_part, ar, chosen, g_raw, m_keep, mc_send, mc_recv, my_send, my_recv, mz_send, mz_recv, mx,
    qx_send, qx_recv, qz_send, qz, qy, qc,
    n_c, n_y, n_z, n_total,
    send_sem, recv_sem, load_sem,
):
    tm, dp, x = lax.axis_index("tm"), lax.axis_index("dp"), lax.axis_index("factor")
    y, c = tm // 4, tm % 2
    z = dp * 2 + (tm // 2) % 2
    group = tm * 4 + dp
    unit = group * 4 + x
    left, right, opposite = (x + 3) % 4, (x + 1) % 4, (x + 2) % 4

    def peer(dx=0, dy=0, dz=0, dc=0):
        return device((x + dx) % 4, (y + dy) % 4, (z + dz) % 8, (c + dc) % 2)

    out_dsts = [
        {"tm": u // 16, "dp": (u // 4) % 4, "factor": u % 4}
        for u in [64 * x + 32 * c + 8 * y + i for i in range(8)]
    ]
    out_srcs = [device(unit // 64, (unit // 8) % 4, i, (unit // 32) % 2) for i in range(8)]
    turn_dsts = [device(i, x, z, c) for i in range(4)]
    turn_srcs = [device(y, i, z, c) for i in range(4)]
    own_unit = 64 * x + 32 * c + 8 * y + z
    out_dst = {"tm": own_unit // 16, "dp": (own_unit // 4) % 4, "factor": own_unit % 4}
    out_src = device(unit // 64, (unit // 8) % 4, unit % 8, (unit // 32) % 2)
    in_unit = [64 * x + 16 * y + 2 * z + h for h in range(2)]
    in_dst = [{"tm": u // 16, "dp": (u // 4) % 4, "factor": u % 4} for u in in_unit]
    in_src = [device(unit // 64, (unit // 16) % 4, (unit // 2) % 8, h) for h in range(2)]

    def same(d):
        return (d["tm"] == tm) & (d["dp"] == dp) & (d["factor"] == x)

    wanted = (
        (valid_hbm, valid_ref), (at_hbm, at_ref), (g_hbm, g_raw), (bi_hbm, bi), (bo_hbm, bo),
        (eo_hbm, eo_ref), (ei_hbm, ei_ref), (prev_in_hbm, prev_in_ref), (prev_out_hbm, prev_out_ref),
    )
    loads = [pltpu.make_async_copy(*pair, load_sem.at[i]) for i, pair in enumerate(wanted)]
    load_valid, load_at, load_g, load_bi, load_bo = loads[:5]
    load_valid.start()
    load_at.start()

    barrier = pltpu.get_barrier_semaphore()
    peers = [peer(dx=i) for i in (1, 2, 3)] + [peer(dy=i) for i in (1, 2, 3)]
    peers += [peer(dz=i) for i in range(1, 8)] + [peer(dc=1)]
    for d in peers:
        pl.semaphore_signal(barrier, inc=1, device_id=d, device_id_type=MESH)
    for d in turn_srcs + out_srcs + in_src:

        @pl.when(jnp.logical_not(same(d)))
        def _():
            pl.semaphore_signal(barrier, inc=1, device_id=d, device_id_type=MESH)

    expected = len(peers)
    for d in turn_dsts + out_dsts + in_dst:
        expected = expected + jnp.where(same(d), 0, 1)

    for load in loads[2:]:
        load.start()
    load_valid.wait()
    load_at.wait()
    length = jnp.sum(valid_ref[...], keepdims=True)
    a_all[x] = jnp.where(
        lax.broadcasted_iota(jnp.int32, (WA, FR), 1) < length, at_ref[...], jnp.zeros((), BF16)
    )
    n_c[0] = jnp.broadcast_to(length.astype(F32), (8, 128))
    qz_send[...] = jnp.zeros_like(qz_send)
    pl.semaphore_wait(barrier, expected)

    count = [0]
    started = []

    def fresh():
        count[0] += 1
        return count[0] - 1

    def send(src, dst, to, k, alone=True):
        copy = pltpu.make_async_remote_copy(
            src_ref=src, dst_ref=dst, send_sem=send_sem.at[k], recv_sem=recv_sem.at[k],
            device_id=to, device_id_type=MESH,
        )
        copy.start()
        if alone:
            started.append(copy)

    def described(ref, k):
        return pltpu.make_async_remote_copy(
            src_ref=ref, dst_ref=ref, send_sem=send_sem.at[k], recv_sem=recv_sem.at[k],
            device_id=peer(dx=1), device_id_type=MESH,
        )

    def landed(dst, k):
        described(dst, k).wait_recv()

    def send_all(pairs, received, k):
        for src, dst, to in pairs:
            send(src, dst, to, k, alone=False)
        started.append(described(received, k))

    def part(buf, shard, h, cols=None):
        rows = buf.shape[1] // 2
        rows = pl.ds(0, buf.shape[1]) if h is None else pl.ds(h * rows, rows)
        return buf.at[shard, rows] if cols is None else buf.at[shard, rows, cols]

    ka = [fresh() for _ in range(6)]
    kg = [fresh() for _ in range(8)]
    near_cols, last_cols = slice(0, 512), slice(512, 640)

    def both(buf, k, to_right, to_left, cols=None):
        for shard, h, i in ((x, to_right, 1), (x, to_left, 3)):
            at = part(buf, shard, h, cols)
            send(at, at, peer(dx=i), k[i // 2])

    def both_landed(buf, k, from_left, from_right, cols=None):
        landed(part(buf, left, from_left, cols), k[0])
        landed(part(buf, right, from_right, cols), k[1])

    def onward(buf, k, cols=None):
        send(part(buf, left, 0, cols), part(buf, left, 0, cols), peer(dx=1), k[0])
        send(part(buf, right, 1, cols), part(buf, right, 1, cols), peer(dx=3), k[1])

    def far_landed(buf, k, cols=None):
        landed(part(buf, opposite, 0, cols), k[0])
        landed(part(buf, opposite, 1, cols), k[1])

    both(a_all, ka[0:2], 0, 1)
    both(a_all, ka[2:4], 1, 0)

    kc, ky, kz = fresh(), fresh(), fresh()
    n_y_others, n_z_others = n_y.at[pl.ds(1, 3)], n_z.at[pl.ds(1, 7)]
    send(n_c.at[0], n_c.at[1], peer(dc=1), kc)

    def count_y():
        landed(n_c.at[1], kc)
        n_y[0] = n_c[0] + n_c[1]
        pairs = [(n_y.at[0], n_y.at[i + 1], peer(dy=i + 1)) for i in range(3)]
        send_all(pairs, n_y_others, ky)

    def count_z():
        landed(n_y_others, ky)
        n_z[0] = n_y[0] + n_y[1] + n_y[2] + n_y[3]
        pairs = [(n_z.at[0], n_z.at[i + 1], peer(dz=i + 1)) for i in range(7)]
        send_all(pairs, n_z_others, kz)

    def count_done():
        landed(n_z_others, kz)
        total = n_z[0]
        for i in range(7):
            total = total + n_z[i + 1]
        n_total[...] = total

    class Scatter:
        def __init__(self, b):
            self.tiles = WIDTHS[b] // 128
            self.keep, self.c_send, self.c_recv = keeps[b], c_sends[b], c_recvs[b]
            self.y_send, self.y_recv = y_sends[b], y_recvs[b]
            self.z_send, self.z_recv = z_sends[b], z_recvs[b]
            self.o_send, self.o_recv = o_sends[b], o_recvs[b]
            self.kc, self.ky, self.kz, self.ko = fresh(), fresh(), fresh(), fresh()
            self.y_others = self.y_recv.at[pl.ds(0, 3)]

        def core(self, half):
            self.c_send[...] = half(1 - c).astype(BF16)
            send(self.c_send, self.c_recv, peer(dc=1), self.kc)
            self.keep[...] = half(c)

        def along_y(self):
            landed(self.c_recv, self.kc)
            total = self.keep[...] + self.c_recv[...].astype(F32)
            self.keep[...] = total
            self.y_send[...] = total.astype(BF16)
            pairs = []
            for i in range(3):
                rows = pl.ds(pl.multiple_of((y + i + 1) % 4 * 80, 16), 80)
                pairs.append((self.y_send.at[rows], self.y_recv.at[i], peer(dy=i + 1)))
            send_all(pairs, self.y_others, self.ky)

        def sum_y(self):
            total = self.keep[pl.ds(pl.multiple_of(y * 80, 16), 80)]
            landed(self.y_others, self.ky)
            for i in range(3):
                total = total + self.y_recv[i].astype(F32)
            return total

        def pack_z(self):
            total = self.sum_y()
            for i in range(8):
                pieces = [
                    total[10 * i : 10 * i + 10, 128 * j : 128 * j + 128] for j in range(self.tiles)
                ]
                pieces = jnp.concatenate(pieces, axis=0).astype(BF16)
                self.z_send[i, : 10 * self.tiles] = pieces

        def along_z(self):
            self.pack_z()
            pairs = [
                (self.z_send.at[(z + i + 1) % 8], self.z_recv.at[i], peer(dz=i + 1))
                for i in range(7)
            ]
            send_all(pairs, self.z_recv, self.kz)

        def done(self):
            total = self.z_send[z].astype(F32)
            landed(self.z_recv, self.kz)
            for i in range(7):
                total = total + self.z_recv[i].astype(F32)
            return total

        def out_copy(self):
            return pltpu.make_async_remote_copy(
                src_ref=self.o_send, dst_ref=self.o_recv, send_sem=send_sem.at[self.ko],
                recv_sem=recv_sem.at[self.ko], device_id=out_dst, device_id_type=MESH,
            )

        def hand_out(self):
            self.o_send[...] = self.done()
            self_dst = same(out_dst)

            @pl.when(self_dst)
            def _():
                self.o_recv[...] = self.o_send[...]

            @pl.when(jnp.logical_not(self_dst))
            def _():
                self.out_copy().start()

        def handed_out(self):
            @pl.when(jnp.logical_not(same(out_src)))
            def _():
                landed(self.o_recv, self.ko)

            return self.o_recv[...]

    class Spread:
        def __init__(self, src, recv, slot, dsts, srcs):
            self.src, self.recv, self.slot, self.dsts, self.srcs = src, recv, slot, dsts, srcs
            self.k = fresh()
            self.self_dst, self.self_src = (
                functools.reduce(jnp.logical_or, [same(d) for d in to]) for to in (dsts, srcs)
            )

        def start(self):
            for i, d in enumerate(self.dsts):

                @pl.when(same(d))
                def _(i=i):
                    self.recv[self.slot] = self.src(i)[...]

                @pl.when(jnp.logical_not(same(d)))
                def _(i=i, d=d):
                    send(self.src(i), self.recv.at[self.slot], d, self.k, alone=False)

        def wait(self, own, act):
            @pl.when(own)
            def _():
                act(described(self.recv.at[pl.ds(0, len(self.dsts) - 1)], self.k))

            @pl.when(jnp.logical_not(own))
            def _():
                act(described(self.recv, self.k))

        def total(self):
            self.wait(self.self_src, lambda copy: copy.wait_recv())
            total = self.recv[0].astype(F32)
            for i in range(1, len(self.srcs)):
                total = total + self.recv[i].astype(F32)
            return total

        def finish(self):
            self.wait(self.self_dst, lambda copy: copy.wait_send())

    class Straight(Scatter):
        def __init__(self, b):
            super().__init__(b)
            self.spread = Spread(lambda i: self.z_send.at[i], l_recv, z, out_dsts, out_srcs)

        def along_z(self):
            self.pack_z()
            self.spread.start()

        def done(self):
            return self.spread.total()

    class Turned(Scatter):
        def __init__(self, b):
            super().__init__(b)
            self.spread = Spread(
                lambda i: self.y_send.at[pl.ds(80 * i, 80)], self.y_recv, y, turn_dsts, turn_srcs
            )

        def along_y(self):
            landed(self.c_recv, self.kc)
            total = self.keep[...] + self.c_recv[...].astype(F32)
            for i in range(4):
                starts = [(j % 2) * 160 + (j // 2) * 40 + 10 * i for j in range(8)]
                pieces = [total[start : start + 10] for start in starts]
                self.y_send[80 * i : 80 * i + 80] = jnp.concatenate(pieces, axis=0).astype(BF16)
            self.spread.start()

        def sum_y(self):
            return self.spread.total()

    in_rows, own_rows, near_rows, second_rows = (Scatter(i) for i in range(4))
    far_rows, last_rows = Straight(4), Turned(5)
    ki_send = [fresh() for _ in range(2)]
    ki = [fresh() for _ in range(2)]

    def in_copy(h):
        return pltpu.make_async_remote_copy(
            src_ref=i_send.at[h], dst_ref=i_recv.at[c], send_sem=send_sem.at[ki_send[h]],
            recv_sem=recv_sem.at[ki[0] + c], device_id=in_dst[h], device_id_type=MESH,
        )

    def hand_in():
        total = in_rows.done()
        for h in range(2):
            for j in range(5):
                lanes = slice(128 * j, 128 * j + 128)
                i_send[h, :5, lanes] = total[10 * j + 5 * h : 10 * j + 5 * h + 5]
        for h in range(2):
            self_dst = same(in_dst[h])

            @pl.when(self_dst)
            def _(h=h):
                i_recv[c] = i_send[h]

            @pl.when(jnp.logical_not(self_dst))
            def _(h=h):
                in_copy(h).start()

    def own_half(h):
        return dot(gt[pl.ds(pl.multiple_of(h * 320, 16), 320)], g_all[x])

    def near_half(cols):
        def half(h):
            rows = gt[pl.ds(pl.multiple_of(h * 320, 16), 320)]
            sides = [dot(rows, g_all[shard, :, cols]) for shard in (left, right)]
            return jnp.concatenate(sides, axis=1)

        return half

    def far_half(h):
        rows = gt[pl.ds(pl.multiple_of(h * 320, 16), 320)]
        return dot(rows, g_all[opposite, :, near_cols])

    def last_half(h):
        rows = [gt[pl.ds(pl.multiple_of(i * 320 + h * 160, 16), 160)] for i in range(2)]
        return dot(jnp.concatenate(rows, axis=0), g_all[opposite, :, last_cols])

    def in_block(h):
        other = a_all[pl.ds(2 * h, 2)].reshape(2 * WA, FR)
        return dot_nt(a_all[x], other)

    load_g.wait()
    g_all[x] = jnp.where(
        lax.broadcasted_iota(jnp.int32, (FR, WG), 0) < length, g_raw[...], jnp.zeros((), BF16)
    )
    gt[...] = g_all[x].T
    own_rows.core(own_half)
    count_y()
    for buf in z_sends:
        buf[...] = jnp.zeros_like(buf)
    mz_send[...] = jnp.zeros_like(mz_send)
    i_send[...] = jnp.zeros_like(i_send)
    own_rows.along_y()
    count_z()
    both_landed(a_all, ka[0:2], 0, 1)
    onward(a_all, ka[4:6])
    both(g_all, kg[0:2], None, None, near_cols)
    load_bi.wait()
    for i in range(4):
        bit[i] = bi[i * WA : (i + 1) * WA].T

    line = lax.broadcasted_iota(jnp.int32, (256, WG), 0)
    slot, at_z = line % 32, line // 32
    source = (at_z % 2) * 320 + (at_z // 2) * 40 + jnp.where(slot >= 10, 150, 0) + slot
    source = jnp.where(slot < 20, source, -WG)
    ahead = lax.broadcasted_iota(jnp.int32, (256, WG), 1) - source
    for i in range(4):
        chosen[i] = (ahead == 10 * i).astype(F32).astype(BF16)
    own_rows.along_z()
    count_done()
    both_landed(a_all, ka[2:4], 1, 0)

    def rotate_near(t, carry):
        rows = pl.ds(pl.multiple_of(t * 320, 16), 320)
        total = dot(bit[x, rows], a_all[x]) + dot(bit[left, rows], a_all[left])
        ar_part[rows] = total + dot(bit[right, rows], a_all[right])
        return carry

    lax.fori_loop(0, 4, rotate_near, 0)
    far_landed(a_all, ka[4:6])

    def cross(h):
        def rotate_far(t, carry):
            rows = pl.ds(pl.multiple_of(h * 640 + t * 320, 16), 320)
            ar[rows] = (ar_part[rows] + dot(bit[opposite, rows], a_all[opposite])).astype(BF16)
            return carry

        lax.fori_loop(0, 2, rotate_far, 0)
        return dot(ar[pl.ds(pl.multiple_of(h * 640, 16), 640)], g_all[x])

    kmc, kmy, kmz, kmx, kqx = fresh(), fresh(), fresh(), [fresh() for _ in range(3)], fresh()
    mc_send[...] = cross(1 - c).astype(BF16)
    send(mc_send, mc_recv, peer(dc=1), kmc)
    m_keep[...] = cross(c)
    both(g_all, kg[2:4], None, None, last_cols)
    landed(mc_recv, kmc)
    total = m_keep[...] + mc_recv[...].astype(F32)
    m_keep[...] = total
    my_send[...] = total.astype(BF16)
    pairs = []
    for i in range(3):
        rows = pl.ds(pl.multiple_of((y + i + 1) % 4 * 160, 16), 160)
        pairs.append((my_send.at[rows], my_recv.at[i], peer(dy=i + 1)))
    send_all(pairs, my_recv, kmy)
    in_rows.core(in_block)
    own_rows.hand_out()
    for load in loads[4:]:
        load.wait()
    in_rows.along_y()
    total = m_keep[pl.ds(pl.multiple_of(y * 160, 16), 160)]
    landed(my_recv, kmy)
    for i in range(3):
        total = total + my_recv[i].astype(F32)
    for i in range(8):
        pieces = [total[20 * i : 20 * i + 20, 128 * j : 128 * j + 128] for j in range(5)]
        mz_send[i, :100] = jnp.concatenate(pieces, axis=0).astype(BF16)
    pairs = [(mz_send.at[(z + i + 1) % 8], mz_recv.at[i], peer(dz=i + 1)) for i in range(7)]
    send_all(pairs, mz_recv, kmz)
    both_landed(g_all, kg[0:2], None, None, near_cols)
    near_rows.core(near_half(near_cols))
    frames = n_total[:1, :1]
    row = lax.broadcasted_iota(jnp.int32, (20, 1280), 0) + (c * 640 + y * 160 + z * 20)
    here = lax.broadcasted_iota(jnp.int32, (20, 1280), 1) == row
    eigen_rows = jnp.concatenate([ei_ref[i : i + 1] for i in range(10)], axis=1)
    eigen_rows = jnp.sum(jnp.where(here, eigen_rows, 0.0), axis=1, keepdims=True)
    eigen_cols = jnp.concatenate([eo_ref[pl.ds(5 * x + i, 1)] for i in range(5)], axis=1)
    scale = eigen_rows * eigen_cols + damping
    total = mz_send[z].astype(F32)
    landed(mz_recv, kmz)
    for i in range(7):
        total = total + mz_recv[i].astype(F32)

    mx[x] = total.astype(BF16)
    for i in range(3):
        send(mx.at[x], mx.at[x], peer(dx=i + 1), kmx[i])
    onward(g_all, kg[4:6], near_cols)
    in_rows.along_z()
    near_rows.along_y()
    both_landed(g_all, kg[2:4], None, None, last_cols)
    second_rows.core(near_half(last_cols))
    near_rows.along_z()
    for i in range(3):
        landed(mx.at[(x + 3 - i) % 4], kmx[i])
    total = jnp.zeros((20, WG), F32)
    for i in range(4):
        pieces = [mx[i, 20 * j : 20 * j + 20] for j in range(5)]
        total = total + dot(jnp.concatenate(pieces, axis=1), bo[i * WG : (i + 1) * WG])
    scaled = (total / frames / scale).astype(BF16)
    kqz = [fresh() for _ in range(7)]
    kqy, kqc = [fresh() for _ in range(3)], fresh()
    turned = dot_nt(scaled, bo[...]).astype(BF16)
    turned = jnp.concatenate([turned[:, WG * i : WG * i + WG] for i in range(4)], axis=0)
    for i in range(4):
        qx_send[i] = dot_nt(turned, chosen[i]).astype(BF16)
    pairs = [(qx_send.at[(x + i + 1) % 4], qx_recv.at[i], peer(dx=i + 1)) for i in range(3)]
    send_all(pairs, qx_recv, kqx)
    onward(g_all, kg[6:8], last_cols)
    second_rows.along_y()
    hand_in()
    near_rows.hand_out()
    far_landed(g_all, kg[4:6], near_cols)
    far_rows.core(far_half)
    total = qx_send[x].astype(F32)
    landed(qx_recv, kqx)
    for i in range(3):
        total = total + qx_recv[i].astype(F32)
    for i in range(8):
        lanes = slice(32 * i, 32 * i + 32)
        pieces = [total[20 * j : 20 * j + 20, lanes] for j in range(4)]
        qz_send[i, :20] = jnp.concatenate(pieces, axis=1).astype(BF16)
    qz[z] = qz_send[z]
    for i in range(7):
        send(qz_send.at[(z + i + 1) % 8], qz.at[z], peer(dz=i + 1), kqz[i])
    second_rows.along_z()
    far_rows.along_y()
    far_landed(g_all, kg[6:8], last_cols)
    last_rows.core(last_half)
    for i in range(7):
        landed(qz.at[(z + 7 - i) % 8], kqz[i])
    for i in range(8):
        qy[y, 20 * i : 20 * i + 20] = qz[i, :20]
    for i in range(3):
        send(qy.at[y], qy.at[y], peer(dy=i + 1), kqy[i])
    second_rows.hand_out()
    far_rows.along_z()
    last_rows.along_y()
    for i in range(3):
        landed(qy.at[(y + 3 - i) % 4], kqy[i])
    qc[c] = qy[...].reshape(640, 128)
    send(qc.at[c], qc.at[c], peer(dc=1), kqc)
    last_rows.along_z()
    landed(qc.at[1 - c], kqc)
    mine = lax.broadcasted_iota(jnp.int32, (16, 128), 0) + (y * 32 + c * 10)
    mine = lax.broadcasted_iota(jnp.int32, (16, 128), 1) == mine
    picked = dot_nt(mine.astype(F32).astype(BF16), qc[...].reshape(1280, 128)).astype(BF16)
    pre_ref[...] = dot_nt(picked, bi[...])[:10].astype(BF16)
    stores = [
        pltpu.make_async_copy(pair[0], pair[1], load_sem.at[9 + i])
        for i, pair in enumerate(((pre_ref, pre_out), (fin_ref, fin_out), (fout_ref, fout_out)))
    ]
    stores[0].start()

    for h in range(2):

        @pl.when(jnp.logical_not(same(in_src[h])))
        def _(h=h):
            landed(i_recv.at[h], ki[h])

        cols = slice(640 * h, 640 * h + 640)
        fin_ref[:, cols] = factor_decay * prev_in_ref[:, cols] + (1.0 - factor_decay) * (
            i_recv[h, :5] / frames
        )
    stores[1].start()
    source = unit // 64

    def write_out(places, total):
        for j, (step, lane) in enumerate(places):
            at = pl.multiple_of(((source + step) % 4) * WG, 128) + lane
            lanes = pl.ds(pl.multiple_of(at, 128), 128)
            fout_ref[:, lanes] = factor_decay * prev_out_ref[:, lanes] + (1.0 - factor_decay) * (
                total[10 * j : 10 * j + 10] / frames
            )

    def tiles(step, cols=None):
        start, stop = (0, WG) if cols is None else (cols.start, cols.stop)
        return [(step, lane) for lane in range(start, stop, 128)]

    write_out(tiles(0), own_rows.handed_out())
    write_out(tiles(3, near_cols) + tiles(1, near_cols), near_rows.handed_out())
    write_out(tiles(3, last_cols) + tiles(1, last_cols), second_rows.handed_out())
    write_out(tiles(2, near_cols), far_rows.done())
    write_out(tiles(2, last_cols), last_rows.done())
    stores[2].start()

    for copy in started:
        copy.wait_send()
    @pl.when(jnp.logical_not(same(out_dst)))
    def _():
        for rows in (own_rows, near_rows, second_rows):
            rows.out_copy().wait_send()

    far_rows.spread.finish()
    last_rows.spread.finish()
    for h in range(2):

        @pl.when(jnp.logical_not(same(in_dst[h])))
        def _(h=h):
            in_copy(h).wait_send()

    for store in stores:
        store.wait()
    assert count[0] <= MESSAGES, count[0]


def handed_on(*refs):
    for i in range(3):
        refs[3 + i][...] = refs[i][...]


def shards(
    activations, gradients, valid_frames, basis_in, basis_out, eigen_in, eigen_out,
    previous_in, previous_out,
):
    vmem = pl.BlockSpec(memory_space=pltpu.VMEM)
    hbm = pl.BlockSpec(memory_space=pl.ANY)
    V = pltpu.VMEM
    results = pl.pallas_call(
        kernel,
        out_shape=(
            jax.ShapeDtypeStruct(previous_in.shape, F32),
            jax.ShapeDtypeStruct(previous_out.shape, F32),
            jax.ShapeDtypeStruct((10, 1280), BF16),
        ),
        in_specs=[hbm] * 9,
        out_specs=(hbm, hbm, hbm),
        scratch_shapes=[
            V((4, WA, FR), BF16), V((4, FR, WG), BF16), V((WG, FR), BF16),
            V((1280, 1280), BF16), V((2560, WG), BF16), V((4, 1280, WA), BF16),
            [V((320, w), F32) for w in WIDTHS], [V((320, w), BF16) for w in WIDTHS],
            [V((320, w), BF16) for w in WIDTHS], [V((320, w), BF16) for w in WIDTHS],
            [V((4, 80, w), BF16) for w in WIDTHS], [V((8, lines_of(w), 128), BF16) for w in WIDTHS],
            [V((7, lines_of(w), 128), BF16) for w in WIDTHS],
            [V((lines_of(w), 128), F32) for w in WIDTHS], [V((lines_of(w), 128), F32) for w in WIDTHS],
            V((8, lines_of(WIDTHS[4]), 128), BF16), V((2, 8, 640), F32), V((2, 8, 640), F32),
            V((WA, FR), BF16), V((8, 128), jnp.int32), V((20, 128), F32), V((10, 128), F32),
            V((5, 1280), F32), V((10, 2560), F32),
            V((5, 1280), F32), V((10, 2560), F32), V((10, 1280), BF16),
            V((1280, FR), F32), V((1280, FR), BF16), V((4, 256, WG), BF16),
            V((FR, WG), BF16),
            V((640, 640), F32), V((640, 640), BF16), V((640, 640), BF16),
            V((640, 640), BF16), V((3, 160, 640), BF16),
            V((8, 112, 128), BF16), V((7, 112, 128), BF16),
            V((4, 112, 128), BF16),
            V((4, 80, 256), BF16), V((3, 80, 256), BF16), V((8, 32, 128), BF16),
            V((8, 32, 128), BF16), V((4, 160, 128), BF16), V((2, 640, 128), BF16),
            V((2, 8, 128), F32), V((4, 8, 128), F32), V((8, 8, 128), F32),
            V((8, 128), F32),
            pltpu.SemaphoreType.DMA((MESSAGES,)), pltpu.SemaphoreType.DMA((MESSAGES,)),
            pltpu.SemaphoreType.DMA((12,)),
        ],
        compiler_params=pltpu.CompilerParams(
            collective_id=0, has_side_effects=True, vmem_limit_bytes=60 * 1024 * 1024
        ),
    )(
        activations.T, gradients, valid_frames.reshape(8, 128), basis_in, basis_out,
        eigen_out.reshape(20, 128), eigen_in.reshape(10, 128), previous_in, previous_out,
    )
    return pl.pallas_call(
        handed_on,
        out_shape=[jax.ShapeDtypeStruct(r.shape, r.dtype) for r in results],
        in_specs=[vmem] * 3,
        out_specs=[vmem] * 3,
    )(*results)


def solution(mesh):
    rows = P(("tm", "dp", "factor"), None)
    in_specs = (
        P(("tm", "dp"), "factor"),
        P(("tm", "dp"), "factor"),
        P(("tm", "dp")),
        P(),
        P(None, "factor"),
        P(),
        P(),
        rows,
        rows,
    )
    return jax.shard_map(
        shards, mesh=mesh, in_specs=in_specs, out_specs=(rows, rows, rows), check_vma=False
    )
```
